256 devices in a mesh: dp: 32 (over x, z), tensor: 8 (over y, core).
Axes of the slice: x: 4, y: 4, z: 8, core: 2. Of those that a mesh axis runs over, the one named last changes fastest.
Arguments:
- tokens: bfloat16 [1024, 6144], P('dp', 'tensor'), may hold values from -32 to 32
- gain_in: float32 [6144], P('tensor'), may hold values from 0.1 to 1.9
- shift_in: float32 [6144], P('tensor'), may hold values from -3 to 3
- up_weight: bfloat16 [6144, 24576], P('tensor', 'dp'), may hold values from -0.078125 to 0.078125
- up_bias: float32 [24576], P('dp'), may hold values from -3 to 3
- down_weight: bfloat16 [24576, 6144], P('dp', 'tensor'), may hold values from -1 to 1
- gain_out: float32 [6144], P('tensor'), may hold values from 0.1 to 1.9
- curvature: float32 [1024, 6144], P('dp', 'tensor'), may hold values from 0.5 to 12
- up_tangent: bfloat16 [6144, 24576], P('tensor', 'dp'), may hold values from -0.078125 to 0.078125
- down_tangent: bfloat16 [24576, 6144], P('dp', 'tensor'), may hold values from -1 to 1
Outputs:
- up_product: float32 [6144, 24576], P('tensor', 'dp')
- down_product: float32 [24576, 6144], P('dp', 'tensor')
The draws below stay inside these ranges and needn't reach their ends.
All inputs are finite; a program needn't handle non-finite values.
Results may differ from the reference program's by a relative error of at most 0.003.
Values may be sent and summed in bfloat16 or wider, within the bound.
A program may use at most 128 MiB of HBM per device.

```python
import math
import jax
import jax.numpy as jnp
from jax import lax

D = 6144
FF = 24576
TOKENS = 1024


def shared_down(key):
    return jax.random.truncated_normal(key, -4.0, 4.0, (FF, D), jnp.float32)


def draw_tokens(key, part):
    key = jax.random.fold_in(key, 11)
    key_scale, key_base, key_rows = jax.random.split(key, 3)
    columns = jnp.arange(D, dtype=jnp.float32) / D
    column_scale = jnp.power(2.0, columns) * jnp.exp(jax.random.uniform(key_scale, (D,), jnp.float32, 0.0, 0.6931))
    base = jax.random.truncated_normal(key_base, -4.0, 4.0, (TOKENS, D), jnp.float32)
    row_scale = jnp.power(2.0, jax.random.uniform(key_rows, (TOKENS, 1), jnp.float32, 0.0, 1.0))
    values = 0.25 * base * column_scale * row_scale
    return values.astype(jnp.bfloat16)


def draw_curvature(key, part):
    key = jax.random.fold_in(key, 23)
    rising = jnp.power(3.0, jnp.arange(D, dtype=jnp.float32) / D)
    base = jnp.exp(jax.random.uniform(key, (TOKENS, D), jnp.float32, -0.6931, 1.3862))
    return (base * rising).astype(jnp.float32)


def draw_down_weight(key, part):
    shared = shared_down(key)
    return (shared * (1.0 / math.sqrt(FF))).astype(jnp.bfloat16)


def draw_down_tangent(key, part):
    shared = shared_down(key)
    key = jax.random.fold_in(key, 37)
    fresh = jax.random.truncated_normal(key, -4.0, 4.0, (FF, D), jnp.float32)
    values = 0.8 * shared + 0.6 * fresh
    return (values * (1.0 / math.sqrt(FF))).astype(jnp.bfloat16)


def level_of(own_key, dims, pieces, least, high):
    loudness, own = 1.0, jax.random.fold_in(own_key, 6)
    for axis_at, blocks in pieces:
        heights = jnp.exp(jax.random.uniform(jax.random.fold_in(own, axis_at), (blocks,), jnp.float32, least / len(pieces), high / len(pieces)))
        loudness = loudness * jnp.repeat(heights, dims[axis_at] // blocks).reshape([-1 if axis == axis_at else 1 for axis in range(len(dims))])
    return loudness


def scatter_about(own_key, dims, deviation, bound, cuts=(), held_as=jnp.bfloat16):
    factor_of = level_of(own_key, dims, cuts, -0.22, 0.18) if cuts else 1.0
    drawn = jax.random.normal(own_key, dims, jnp.float32) * deviation * factor_of
    return jnp.minimum(jnp.maximum(drawn, -bound), bound).astype(held_as)


def setup_inputs(seed: int = 0) -> dict:
    streams_of = jax.random.split(jax.random.key(seed), 11)
    tokens = draw_tokens(jax.random.fold_in(streams_of[10], 71), 0)
    gain_in = jnp.clip(1.0 + 0.18 * jax.random.normal(streams_of[1], (D,), jnp.float32), 0.1, 1.9)
    shift_in = scatter_about(streams_of[2], (D,), 0.5, 3.0, ((0, 8),), jnp.float32)
    up_weight = scatter_about(streams_of[3], (D, FF), D ** -0.5, 0.078125, ((0, 8), (1, 32)))
    up_bias = scatter_about(streams_of[4], (FF,), 0.5, 3.0, ((0, 32),), jnp.float32)
    down_weight = draw_down_weight(jax.random.fold_in(streams_of[10], 71), 0)
    gain_out = jnp.clip(1.0 + 0.18 * jax.random.normal(streams_of[6], (D,), jnp.float32), 0.1, 1.9)
    curvature = draw_curvature(jax.random.fold_in(streams_of[10], 71), 0)
    up_tangent = scatter_about(streams_of[8], (D, FF), D ** -0.5, 0.078125, ((0, 8), (1, 32)))
    down_tangent = draw_down_tangent(jax.random.fold_in(streams_of[10], 71), 0)
    return dict(tokens=tokens, gain_in=gain_in, shift_in=shift_in, up_weight=up_weight, up_bias=up_bias, down_weight=down_weight, gain_out=gain_out, curvature=curvature, up_tangent=up_tangent, down_tangent=down_tangent)


epsilon = 1e-05
root_half = 0.7071067811865476
inv_root_two_pi = 0.3989422804014327

def gelu_value(values):
    return 0.5 * values * (1.0 + lax.erf(values * root_half))

def gelu_slope(values):
    return 0.5 * (1.0 + lax.erf(values * root_half)) + values * jnp.exp(-0.5 * values * values) * inv_root_two_pi

def reference(tokens, gain_in, shift_in, up_weight, up_bias, down_weight, gain_out, curvature, up_tangent, down_tangent):
    source = tokens.astype(jnp.float32)
    center_in = lax.optimization_barrier(jnp.mean(source, axis=1, keepdims=True))
    spread_in = lax.optimization_barrier(jnp.mean(jnp.square(source - center_in), axis=1, keepdims=True))
    normed = ((source - center_in) * lax.rsqrt(spread_in + epsilon) * gain_in + shift_in).astype(jnp.bfloat16)
    pre_full = jnp.dot(normed, up_weight, preferred_element_type=jnp.float32) + up_bias
    tangent_pre = jnp.dot(normed, up_tangent, preferred_element_type=jnp.float32)
    hidden = gelu_value(pre_full).astype(jnp.bfloat16)
    slope_full = gelu_slope(pre_full)
    hidden_tangent = (slope_full * tangent_pre).astype(jnp.bfloat16)
    slope_kept = lax.optimization_barrier(slope_full.astype(jnp.bfloat16))
    output = source + jnp.dot(hidden, down_weight, preferred_element_type=jnp.float32)
    output_tangent = jnp.dot(hidden_tangent, down_weight, preferred_element_type=jnp.float32) + jnp.dot(hidden, down_tangent, preferred_element_type=jnp.float32)
    center_out = lax.optimization_barrier(jnp.mean(output, axis=1, keepdims=True))
    spread_out = lax.optimization_barrier(jnp.mean(jnp.square(output - center_out), axis=1, keepdims=True))
    inverse_out = lax.rsqrt(spread_out + epsilon)
    normal_out = (output - center_out) * inverse_out
    normal_tangent = (output_tangent - lax.optimization_barrier(jnp.mean(output_tangent, axis=1, keepdims=True)) - normal_out * lax.optimization_barrier(jnp.mean(normal_out * output_tangent, axis=1, keepdims=True))) * inverse_out
    weighted = gain_out * gain_out * curvature * normal_tangent
    cotangent = ((weighted - lax.optimization_barrier(jnp.mean(weighted, axis=1, keepdims=True)) - normal_out * lax.optimization_barrier(jnp.mean(normal_out * weighted, axis=1, keepdims=True))) * inverse_out).astype(jnp.bfloat16)
    down_product = jnp.dot(hidden.T, cotangent, preferred_element_type=jnp.float32)
    back_hidden = jnp.dot(cotangent, down_weight.T, preferred_element_type=jnp.float32)
    grad_pre = (back_hidden * slope_kept.astype(jnp.float32)).astype(jnp.bfloat16)
    up_product = jnp.dot(normed.T, grad_pre, preferred_element_type=jnp.float32)
    return (up_product, down_product)
```

```python
import functools

import jax
import jax.numpy as jnp
from jax import lax
from jax.experimental import pallas as pl
from jax.experimental.pallas import tpu as pltpu
from jax.sharding import PartitionSpec as P

D = 6144
epsilon = 1e-05
root_half = 0.7071067811865476
inv_root_two_pi = 0.3989422804014327

f32 = jnp.float32
bf16 = jnp.bfloat16
MESH = pl.DeviceIdType.MESH

NX, NZ, NY = 4, 8, 4
OWN = 16
QUARTER = NZ * OWN
SHARE = QUARTER // NY
ROWS = NX * QUARTER
W = 768
TILE = 256
TILES = W // TILE
X_OFFSETS = (0, 1, 3, 2)
Z_NEAR = (1, 7, 2, 6, 3, 5, 4)
Z_FAR = (4, 3, 5, 2, 6, 1, 7)
Y_ORDER = (2, 1, 3)

N_SEND = 160
N_RECV = 120
N_LOCAL = 24


def dot(a, b):
    return jnp.dot(a, b, preferred_element_type=f32)


def dot_last(a, b):
    return lax.dot_general(a, b, (((1,), (1,)), ((), ())), preferred_element_type=f32)


def dot_first(a, b):
    return lax.dot_general(a, b, (((0,), (0,)), ((), ())), preferred_element_type=f32)


def columns(values):
    lane = lax.broadcasted_iota(jnp.int32, (OWN, 128), 1)
    out = jnp.zeros((OWN, 128), f32)
    for at, value in enumerate(values):
        out = jnp.where(lane == at, value, out)
    return out


def row_sum(pair):
    return jnp.sum(pair[0] + pair[1], axis=1, keepdims=True)


def kernel(
    tokens, gain_in, shift_in, up_weight, up_bias, down_weight, gain_out, curvature, up_tangent, down_tangent,
    up_out, down_out,
    w_up, w_ut, w_dn, w_dt, tok, curv, gin_x, sin_x, gout_x,
    stat_a, stat_b, normed, normed_x, part_f, part_s, part_r, part_own,
    both, hidden_x, slope, own_x, out_s, out_r, sum_s, sum_r,
    cot, cot_x, back_f, back_s, back_r, back_own, grad, grad_x, stage,
    send_sem, recv_sem, local_sem,
):
    d, t = lax.axis_index("dp"), lax.axis_index("tensor")
    x, z = d // NZ, lax.rem(d, NZ)
    y, c = t // 2, lax.rem(t, 2)
    other = 1 - c

    def at_x(k):
        return (lax.rem(x + k, NX) * NZ + z, t)

    def at_z(k):
        return (x * NZ + lax.rem(z + k, NZ), t)

    def at_y(k):
        return (d, lax.rem(y + k, NY) * 2 + c)

    sibling = (d, y * 2 + other)
    sends, locals_, counts = [], [], {"send": 0, "recv": 0, "local": 0}

    def fresh(kind, n=1):
        at = counts[kind]
        counts[kind] += n
        return at

    def copy_to(src, dst, device, slot):
        copy = pltpu.make_async_remote_copy(
            src_ref=src, dst_ref=dst, send_sem=send_sem.at[fresh("send")],
            recv_sem=recv_sem.at[slot], device_id=device, device_id_type=MESH,
        )
        copy.start()
        sends.append(copy)

    def arrived(dst, slot):
        pltpu.make_async_remote_copy(
            src_ref=dst, dst_ref=dst, send_sem=send_sem.at[0],
            recv_sem=recv_sem.at[slot], device_id=sibling, device_id_type=MESH,
        ).wait_recv()

    def copy_here(src, dst):
        copy = pltpu.make_async_copy(src, dst, local_sem.at[fresh("local")])
        copy.start()
        return copy

    own_rows = pl.ds(pl.multiple_of(c * OWN, OWN), OWN)
    their_rows = pl.ds(pl.multiple_of(other * OWN, OWN), OWN)
    tok_here = copy_here(tokens.at[own_rows], tok.at[c])
    curv_here = copy_here(curvature.at[own_rows], curv.at[c])
    up_here = [copy_here(up_weight, w_up.at[c]), copy_here(up_tangent, w_ut.at[c])]
    down_here = [copy_here(down_weight, w_dn.at[c]), copy_here(down_tangent, w_dt.at[c])]
    barrier = pltpu.get_barrier_semaphore()
    peers = [sibling] + [at_x(k) for k in range(1, NX)] + [at_z(k) for k in range(1, NZ)] + [at_y(k) for k in range(1, NY)]
    for peer in peers:
        pl.semaphore_signal(barrier, inc=1, device_id=peer, device_id_type=MESH)
    pl.semaphore_wait(barrier, len(peers))

    tok_slot, params_slot, curv_slot = fresh("recv"), fresh("recv", 3), fresh("recv")
    up_slot, down_slot = fresh("recv", 2), fresh("recv", 2)
    copy_to(tokens.at[their_rows], tok.at[c], sibling, tok_slot)
    copy_to(gain_in, gin_x, sibling, params_slot)
    copy_to(shift_in, sin_x, sibling, params_slot + 1)
    copy_to(gain_out, gout_x, sibling, params_slot + 2)
    copy_to(up_weight, w_up.at[c], sibling, up_slot)
    copy_to(up_tangent, w_ut.at[c], sibling, up_slot + 1)
    copy_to(curvature.at[their_rows], curv.at[c], sibling, curv_slot)
    copy_to(down_weight, w_dn.at[c], sibling, down_slot)
    copy_to(down_tangent, w_dt.at[c], sibling, down_slot + 1)

    tok_here.wait()
    arrived(tok.at[other], tok_slot)
    source = tok[...].astype(f32)
    total = row_sum(source)
    spread = source - (total / (2 * W))[None]
    stat_a[0] = columns([total, row_sum(spread * spread)])
    stat_slot = fresh("recv", 3)
    for k in Y_ORDER:
        copy_to(stat_a.at[0], stat_a.at[k], at_y(k), stat_slot + k - 1)
    arrived(gin_x, params_slot)
    arrived(sin_x, params_slot + 1)
    arrived(gout_x, params_slot + 2)

    def by_half(mine, theirs):
        mine, theirs = mine[...].reshape(1, W), theirs[...].reshape(1, W)
        first = jnp.where(c == 0, mine, theirs)
        second = jnp.where(c == 0, theirs, mine)
        return jnp.stack([first, second])

    gain, shift = by_half(gain_in, gin_x), by_half(shift_in, sin_x)
    for k in range(1, NY):
        arrived(stat_a.at[k], stat_slot + k - 1)
    totals = [stat_a[k][:, 0:1] for k in range(NY)]
    center = (totals[0] + totals[1] + totals[2] + totals[3]) / D
    variance = jnp.zeros_like(center)
    for k in range(NY):
        off = totals[k] / (2 * W) - center
        variance = variance + stat_a[k][:, 1:2] + (2 * W) * (off * off)
    inverse = lax.rsqrt(variance / D + epsilon)
    block = pl.ds(pl.multiple_of(x * QUARTER + z * OWN, OWN), OWN)
    normed[:, block] = ((source - center[None]) * inverse[None] * gain + shift).astype(bf16)

    def rows_of(k):
        return pl.multiple_of(lax.rem(x + X_OFFSETS[k], NX) * QUARTER, QUARTER)

    def gather_start(array):
        z_slot, x_slot = fresh("recv", NZ), fresh("recv", NX)
        for k in Z_FAR:
            copy_to(array.at[:, block], array.at[:, block], at_z(k), z_slot + k)
        for k in (2, 1, 3):
            copy_to(array.at[:, block], array.at[:, block], at_x(k), x_slot + k)
        for k in Z_NEAR:
            from_z = lax.rem(z + NZ - k, NZ)
            landed = pl.ds(pl.multiple_of(x * QUARTER + from_z * OWN, OWN), OWN)
            arrived(array.at[:, landed], z_slot + k)
            for j in (2, 1, 3):
                copy_to(array.at[:, landed], array.at[:, landed], at_x(j), x_slot + j)
        return x_slot

    def gather_wait(array, x_slot, k):
        if k > 0:
            step = (NX - X_OFFSETS[k]) % NX
            arrived(array.at[:, pl.ds(rows_of(k), QUARTER)], x_slot + step)

    normed_slot = gather_start(normed)

    share_slot = fresh("recv", 12)
    both_slot = fresh("recv", 12)
    normed_x_slot, hidden_x_slot = fresh("recv", 4), fresh("recv", 4)
    cot_x_slot, grad_x_slot = fresh("recv", 4), fresh("recv", 4)
    out_slot = fresh("recv", NX)

    def up_step(k):
        gather_wait(normed, normed_slot, k)
        at = rows_of(k)
        rows = pl.ds(at, QUARTER)
        copy_to(normed.at[other, rows], normed_x.at[rows], sibling, normed_x_slot + k)
        if k == 0:
            for copy in up_here:
                copy.wait()
            arrived(w_up.at[other], up_slot)
            arrived(w_ut.at[other], up_slot + 1)
        left, right = normed[0, rows], normed[1, rows]

        @pl.loop(0, TILES)
        def _(n):
            cols = pl.ds(pl.multiple_of(n * TILE, TILE), TILE)
            part_f[0, :, cols] = dot(left, w_up[0, :, cols]) + dot(right, w_up[1, :, cols])
            part_f[1, :, cols] = dot(left, w_ut[0, :, cols]) + dot(right, w_ut[1, :, cols])

        for j in Y_ORDER:
            theirs = pl.ds(pl.multiple_of(lax.rem(y + j, NY) * SHARE, SHARE), SHARE)
            part_s[k, j - 1] = part_f[:, theirs].astype(bf16)
            copy_to(part_s.at[k, j - 1], part_r.at[k, j - 1], at_y(j), share_slot + k * 3 + j - 1)
        part_own[k] = part_f[:, pl.ds(pl.multiple_of(y * SHARE, SHARE), SHARE)]

    def share_rows(k, who):
        return pl.ds(pl.multiple_of(rows_of(k) + who * SHARE, SHARE), SHARE)

    def act_step(k):
        sums = part_own[k]
        for j in range(1, NY):
            arrived(part_r.at[k, j - 1], share_slot + k * 3 + j - 1)
            sums = sums + part_r[k, j - 1].astype(f32)
        pre = sums[0] + up_bias[...].reshape(1, W)
        phi = 0.5 * (1.0 + lax.erf(pre * root_half))
        derivative = phi + pre * jnp.exp(-0.5 * pre * pre) * inv_root_two_pi
        rows = share_rows(k, y)
        both[0, rows] = (pre * phi).astype(bf16)
        both[1, rows] = (derivative * sums[1]).astype(bf16)
        slope[k] = derivative.astype(bf16)
        for j in Y_ORDER:
            copy_to(both.at[:, rows], both.at[:, rows], at_y(j), both_slot + k * 3 + j - 1)

    def down_step(k):
        for j in range(1, NY):
            arrived(both.at[:, share_rows(k, lax.rem(y + NY - j, NY))], both_slot + k * 3 + j - 1)
        rows = pl.ds(rows_of(k), QUARTER)
        copy_to(both.at[0, rows], hidden_x.at[rows], sibling, hidden_x_slot + k)
        if k == 0:
            for copy in down_here:
                copy.wait()
            arrived(w_dn.at[other], down_slot)
            arrived(w_dt.at[other], down_slot + 1)
        hidden, hidden_tangent = both[0, rows], both[1, rows]

        @pl.loop(0, TILES)
        def _(n):
            cols = pl.ds(pl.multiple_of(n * TILE, TILE), TILE)
            for f in range(2):
                weight = w_dn[f, :, cols]
                primal = dot(hidden, weight)
                tangent = dot(hidden_tangent, weight) + dot(hidden, w_dt[f, :, cols])
                if k == 0:
                    own_x[0, f, :, cols] = primal
                    own_x[1, f, :, cols] = tangent
                else:
                    out_s[k - 1, 0, f, :, cols] = primal.astype(bf16)
                    out_s[k - 1, 1, f, :, cols] = tangent.astype(bf16)

        if k > 0:
            step = X_OFFSETS[k]
            copy_to(out_s.at[k - 1], out_r.at[step - 1], at_x(step), out_slot + step)

    up_step(0)
    up_step(1)
    up_step(2)
    act_step(0)
    up_step(3)
    act_step(1)
    down_step(0)
    act_step(2)
    down_step(1)
    act_step(3)
    down_step(2)
    down_step(3)

    for step in range(1, NX):
        arrived(out_r.at[step - 1], out_slot + step)

    def summed(who):
        rows = pl.ds(pl.multiple_of(who * OWN, OWN), OWN)
        value = own_x[:, :, rows]
        for step in range(1, NX):
            value = value + out_r[step - 1, :, :, rows].astype(f32)
        return value

    sum_slot = fresh("recv", NZ)
    for k in Z_FAR:
        sum_s[k - 1] = summed(lax.rem(z + k, NZ)).astype(bf16)
        copy_to(sum_s.at[k - 1], sum_r.at[k - 1], at_z(k), sum_slot + k)
    outputs = summed(z)
    arrived(curv.at[other], curv_slot)
    curv_here.wait()
    gain = by_half(gain_out, gout_x)
    factor = gain * gain * curv[...]
    for k in Z_NEAR:
        arrived(sum_r.at[k - 1], sum_slot + k)
        outputs = outputs + sum_r[k - 1].astype(f32)

    output = tok[...].astype(f32) + outputs[0]
    tangent = outputs[1]
    total = row_sum(output)
    around = output - (total / (2 * W))[None]
    factor_around = factor * around
    stat_b[0] = columns([
        total, row_sum(around * around), row_sum(tangent), row_sum(around * tangent),
        row_sum(factor), row_sum(factor_around), row_sum(factor_around * around),
        row_sum(factor * tangent), row_sum(factor_around * tangent),
    ])
    stat_slot = fresh("recv", 3)
    for k in Y_ORDER:
        copy_to(stat_b.at[0], stat_b.at[k], at_y(k), stat_slot + k - 1)
    for k in range(1, NY):
        arrived(stat_b.at[k], stat_slot + k - 1)
    stats = [[stat_b[k][:, i:i + 1] for i in range(9)] for k in range(NY)]
    center = (stats[0][0] + stats[1][0] + stats[2][0] + stats[3][0]) / D
    zero = jnp.zeros_like(center)
    square, sum_t, dot_t, f_0, f_1, f_2, ft_0, ft_1 = (zero,) * 8
    for s in stats:
        off = s[0] / (2 * W) - center
        square = square + s[1] + (2 * W) * (off * off)
        sum_t = sum_t + s[2]
        dot_t = dot_t + s[3] + off * s[2]
        f_0 = f_0 + s[4]
        f_1 = f_1 + s[5] + off * s[4]
        f_2 = f_2 + s[6] + 2.0 * off * s[5] + off * off * s[4]
        ft_0 = ft_0 + s[7]
        ft_1 = ft_1 + s[8] + off * s[7]
    inverse = lax.rsqrt(square / D + epsilon)
    mean_t = sum_t / D
    mean_nt = dot_t * inverse / D
    fn_1 = f_1 * inverse
    mean_w = (ft_0 - mean_t * f_0 - mean_nt * fn_1) * inverse / D
    mean_nw = (ft_1 * inverse - mean_t * fn_1 - mean_nt * (f_2 * inverse * inverse)) * inverse / D
    normal = (output - center[None]) * inverse[None]
    weighted = factor * ((tangent - mean_t[None] - normal * mean_nt[None]) * inverse[None])
    cot[:, block] = ((weighted - mean_w[None] - normal * mean_nw[None]) * inverse[None]).astype(bf16)

    cot_slot = gather_start(cot)
    back_slot = fresh("recv", 12)
    grad_slot = fresh("recv", 12)

    def back_step(k):
        gather_wait(cot, cot_slot, k)
        rows = pl.ds(rows_of(k), QUARTER)
        copy_to(cot.at[other, rows], cot_x.at[rows], sibling, cot_x_slot + k)
        left, right = cot[0, rows], cot[1, rows]

        @pl.loop(0, TILES)
        def _(n):
            units = pl.ds(pl.multiple_of(n * TILE, TILE), TILE)
            back_f[:, units] = dot_last(left, w_dn[0, units]) + dot_last(right, w_dn[1, units])

        for j in Y_ORDER:
            theirs = pl.ds(pl.multiple_of(lax.rem(y + j, NY) * SHARE, SHARE), SHARE)
            back_s[k, j - 1] = back_f[theirs].astype(bf16)
            copy_to(back_s.at[k, j - 1], back_r.at[k, j - 1], at_y(j), back_slot + k * 3 + j - 1)
        back_own[k] = back_f[pl.ds(pl.multiple_of(y * SHARE, SHARE), SHARE)]

    def grad_step(k):
        sums = back_own[k]
        for j in range(1, NY):
            arrived(back_r.at[k, j - 1], back_slot + k * 3 + j - 1)
            sums = sums + back_r[k, j - 1].astype(f32)
        rows = share_rows(k, y)
        grad[rows] = (sums * slope[k].astype(f32)).astype(bf16)
        for j in Y_ORDER:
            copy_to(grad.at[rows], grad.at[rows], at_y(j), grad_slot + k * 3 + j - 1)

    def swap_step(k):
        for j in range(1, NY):
            arrived(grad.at[share_rows(k, lax.rem(y + NY - j, NY))], grad_slot + k * 3 + j - 1)
        rows = pl.ds(rows_of(k), QUARTER)
        copy_to(grad.at[rows], grad_x.at[rows], sibling, grad_x_slot + k)

    def product(first, first_x, second, second_x, result, slot):
        copies = []
        for n in range(TILES):
            part = pl.ds(n * TILE, TILE)
            stage[slot, part] = dot_first(first(part), second[...]) + dot_first(first_x(part), second_x[...])
            copies.append(copy_here(stage.at[slot, part], result.at[part]))
        return copies

    back_step(0)
    back_step(1)
    back_step(2)
    grad_step(0)
    back_step(3)
    grad_step(1)
    grad_step(2)
    grad_step(3)
    everything = pl.ds(0, ROWS)
    for k in range(NX):
        theirs = pl.ds(rows_of(k), QUARTER)
        arrived(hidden_x.at[theirs], hidden_x_slot + k)
        arrived(cot_x.at[theirs], cot_x_slot + k)
        arrived(normed_x.at[theirs], normed_x_slot + k)
    written = product(
        lambda part: both[0, :, part], lambda part: hidden_x[:, part], cot.at[c], cot_x, down_out, 0,
    )
    for k in range(NX):
        swap_step(k)
    for k in range(NX):
        arrived(grad_x.at[pl.ds(rows_of(k), QUARTER)], grad_x_slot + k)
    written += product(
        lambda part: normed[c, :, part], lambda part: normed_x[:, part], grad, grad_x, up_out, 1,
    )
    for copy in written:
        copy.wait()
    for copy in sends:
        copy.wait_send()


def on_device(*args):
    any_ = pl.BlockSpec(memory_space=pl.ANY)
    vmem = pl.BlockSpec(memory_space=pltpu.VMEM)
    scratch = [
        ((2, W, W), bf16), ((2, W, W), bf16), ((2, W, W), bf16), ((2, W, W), bf16),
        ((2, OWN, W), bf16), ((2, OWN, W), f32), ((W,), f32), ((W,), f32), ((W,), f32),
        ((NY, OWN, 128), f32), ((NY, OWN, 128), f32),
        ((2, ROWS, W), bf16), ((ROWS, W), bf16),
        ((2, QUARTER, W), f32), ((NX, 3, 2, SHARE, W), bf16), ((NX, 3, 2, SHARE, W), bf16), ((NX, 2, SHARE, W), f32),
        ((2, ROWS, W), bf16), ((ROWS, W), bf16), ((NX, SHARE, W), bf16),
        ((2, 2, QUARTER, W), f32), ((3, 2, 2, QUARTER, W), bf16), ((3, 2, 2, QUARTER, W), bf16),
        ((NZ - 1, 2, 2, OWN, W), bf16), ((NZ - 1, 2, 2, OWN, W), bf16),
        ((2, ROWS, W), bf16), ((ROWS, W), bf16),
        ((QUARTER, W), f32), ((NX, 3, SHARE, W), bf16), ((NX, 3, SHARE, W), bf16), ((NX, SHARE, W), f32),
        ((ROWS, W), bf16), ((ROWS, W), bf16), ((2, W, W), f32),
    ]
    return pl.pallas_call(
        kernel,
        out_shape=(jax.ShapeDtypeStruct((W, W), f32), jax.ShapeDtypeStruct((W, W), f32)),
        in_specs=[any_, vmem, vmem, any_, vmem, any_, vmem, any_, any_, any_],
        out_specs=(any_, any_),
        scratch_shapes=[pltpu.VMEM(shape, dtype) for shape, dtype in scratch]
        + [pltpu.SemaphoreType.DMA((N_SEND,)), pltpu.SemaphoreType.DMA((N_RECV,)), pltpu.SemaphoreType.DMA((N_LOCAL,))],
        compiler_params=pltpu.CompilerParams(
            collective_id=0, has_side_effects=True, vmem_limit_bytes=60 * 2**20
        ),
        cost_estimate=pl.CostEstimate(flops=9663676416, bytes_accessed=9437184, transcendentals=262144),
        name="gauss_newton",
    )(*args)


def solution(mesh):
    return jax.shard_map(
        on_device,
        mesh=mesh,
        in_specs=(
            P("dp", "tensor"),
            P("tensor"),
            P("tensor"),
            P("tensor", "dp"),
            P("dp"),
            P("dp", "tensor"),
            P("tensor"),
            P("dp", "tensor"),
            P("tensor", "dp"),
            P("dp", "tensor"),
        ),
        out_specs=(P("tensor", "dp"), P("dp", "tensor")),
        check_vma=False,
    )
```

```python
import functools

import jax
import jax.numpy as jnp
from jax import lax
from jax.experimental import pallas as pl
from jax.experimental.pallas import tpu as pltpu
from jax.sharding import PartitionSpec as P

D = 6144
epsilon = 1e-05
root_half = 0.7071067811865476
inv_root_two_pi = 0.3989422804014327

f32 = jnp.float32
bf16 = jnp.bfloat16
MESH = pl.DeviceIdType.MESH

NX, NZ, NY = 4, 8, 4
OWN = 16
GROUP = NX * OWN
ROWS = NZ * GROUP
W = 768
TILE = 256
TILES = W // TILE
FORWARD = ((1, 7), (4,), (3, 5), (2, 6), (0,))
BACKWARD = ((0,), (1, 7), (2, 6), (3, 5), (4,))
NEAR = (1, 7)
FAR = (4, 3, 5, 2, 6)
J_ORDER = (2, 1, 3)

N_SEND = 320
N_RECV = 400
N_LOCAL = 24


def dot(a, b):
    return jnp.dot(a, b, preferred_element_type=f32)


def dot_last(a, b):
    return lax.dot_general(a, b, (((1,), (1,)), ((), ())), preferred_element_type=f32)


def dot_first(a, b):
    return lax.dot_general(a, b, (((0,), (0,)), ((), ())), preferred_element_type=f32)


def columns(values):
    lane = lax.broadcasted_iota(jnp.int32, (OWN, 128), 1)
    out = jnp.zeros((OWN, 128), f32)
    for at, value in enumerate(values):
        out = jnp.where(lane == at, value, out)
    return out


def row_sum(pair):
    return jnp.sum(pair[0] + pair[1], axis=1, keepdims=True)


def kernel(
    tokens, gain_in, shift_in, up_weight, up_bias, down_weight, gain_out, curvature, up_tangent, down_tangent,
    up_out, down_out,
    w_up, w_ut, w_dn, w_dt, tok, curv, gin_x, sin_x, gout_x,
    stat_a, stat_b, normed, normed_x, part_f, part_s, part_r, part_own,
    both, hidden_x, slope, out_f, raw_s, raw_r, own_x, out_s, out_r, sum_s, sum_r,
    cot, cot_x, back_f, back_s, back_r, back_own, grad, grad_x, stage,
    send_sem, recv_sem, local_sem,
):
    d, t = lax.axis_index("dp"), lax.axis_index("tensor")
    x, z = d // NZ, lax.rem(d, NZ)
    y, c = t // 2, lax.rem(t, 2)
    other = 1 - c

    def at_x(k):
        return (lax.rem(x + k, NX) * NZ + z, t)

    def at_z(k):
        return (x * NZ + lax.rem(z + k, NZ), t)

    def at_y(k):
        return (d, lax.rem(y + k, NY) * 2 + c)

    sibling = (d, y * 2 + other)
    sends, locals_, counts = [], [], {"send": 0, "recv": 0, "local": 0}

    def fresh(kind, n=1):
        at = counts[kind]
        counts[kind] += n
        return at

    def copy_to(src, dst, device, slot):
        copy = pltpu.make_async_remote_copy(
            src_ref=src, dst_ref=dst, send_sem=send_sem.at[fresh("send")],
            recv_sem=recv_sem.at[slot], device_id=device, device_id_type=MESH,
        )
        copy.start()
        sends.append(copy)

    def arrived(dst, slot):
        pltpu.make_async_remote_copy(
            src_ref=dst, dst_ref=dst, send_sem=send_sem.at[0],
            recv_sem=recv_sem.at[slot], device_id=sibling, device_id_type=MESH,
        ).wait_recv()

    def copy_here(src, dst):
        copy = pltpu.make_async_copy(src, dst, local_sem.at[fresh("local")])
        copy.start()
        return copy

    own_rows = pl.ds(pl.multiple_of(c * OWN, OWN), OWN)
    their_rows = pl.ds(pl.multiple_of(other * OWN, OWN), OWN)
    tok_here = copy_here(tokens.at[own_rows], tok.at[c])
    curv_here = copy_here(curvature.at[own_rows], curv.at[c])
    up_here = [copy_here(up_weight, w_up.at[c]), copy_here(up_tangent, w_ut.at[c])]
    down_here = [copy_here(down_weight, w_dn.at[c]), copy_here(down_tangent, w_dt.at[c])]
    barrier = pltpu.get_barrier_semaphore()
    peers = [sibling] + [at_x(k) for k in range(1, NX)] + [at_z(k) for k in range(1, NZ)] + [at_y(k) for k in range(1, NY)]
    for peer in peers:
        pl.semaphore_signal(barrier, inc=1, device_id=peer, device_id_type=MESH)
    pl.semaphore_wait(barrier, len(peers))

    tok_slot, params_slot, curv_slot = fresh("recv"), fresh("recv", 3), fresh("recv")
    up_slot, down_slot = fresh("recv", 2), fresh("recv", 2)
    copy_to(tokens.at[their_rows], tok.at[c], sibling, tok_slot)
    copy_to(gain_in, gin_x, sibling, params_slot)
    copy_to(shift_in, sin_x, sibling, params_slot + 1)
    copy_to(gain_out, gout_x, sibling, params_slot + 2)
    copy_to(up_weight, w_up.at[c], sibling, up_slot)
    copy_to(up_tangent, w_ut.at[c], sibling, up_slot + 1)
    copy_to(curvature.at[their_rows], curv.at[c], sibling, curv_slot)
    copy_to(down_weight, w_dn.at[c], sibling, down_slot)
    copy_to(down_tangent, w_dt.at[c], sibling, down_slot + 1)

    tok_here.wait()
    arrived(tok.at[other], tok_slot)
    source = tok[...].astype(f32)
    total = row_sum(source)
    spread = source - (total / (2 * W))[None]
    stat_a[0] = columns([total, row_sum(spread * spread)])
    stat_slot = fresh("recv", 3)
    for k in J_ORDER:
        copy_to(stat_a.at[0], stat_a.at[k], at_y(k), stat_slot + k - 1)
    arrived(gin_x, params_slot)
    arrived(sin_x, params_slot + 1)
    arrived(gout_x, params_slot + 2)

    def by_half(mine, theirs):
        mine, theirs = mine[...].reshape(1, W), theirs[...].reshape(1, W)
        first = jnp.where(c == 0, mine, theirs)
        second = jnp.where(c == 0, theirs, mine)
        return jnp.stack([first, second])

    gain, shift = by_half(gain_in, gin_x), by_half(shift_in, sin_x)
    for k in range(1, NY):
        arrived(stat_a.at[k], stat_slot + k - 1)
    totals = [stat_a[k][:, 0:1] for k in range(NY)]
    center = (totals[0] + totals[1] + totals[2] + totals[3]) / D
    variance = jnp.zeros_like(center)
    for k in range(NY):
        off = totals[k] / (2 * W) - center
        variance = variance + stat_a[k][:, 1:2] + (2 * W) * (off * off)
    inverse = lax.rsqrt(variance / D + epsilon)
    def group(k):
        return pl.ds(pl.multiple_of(lax.rem(z + NZ + k, NZ) * GROUP, GROUP), GROUP)

    def block_of(j, k):
        first = lax.rem(z + NZ + k, NZ) * GROUP + lax.rem(x + NX + j, NX) * OWN
        return pl.ds(pl.multiple_of(first, OWN), OWN)

    block = block_of(0, 0)
    normed[:, block] = ((source - center[None]) * inverse[None] * gain + shift).astype(bf16)

    def gather_start(array, far):
        def send(rows, device, slot):
            copy_to(array.at[:, rows], array.at[:, rows], device, slot)

        z_slot, x_slot = fresh("recv", NZ), fresh("recv", NX)
        near_slot, far_slot = fresh("recv", NZ * NX), fresh("recv", NZ * NX)
        for j in J_ORDER:
            send(block, at_x(j), x_slot + j)
        for k in NEAR + far:
            send(block, at_z(k), z_slot + k)
        for j in (1, 3, 2):
            rows = block_of(-j, 0)
            arrived(array.at[:, rows], x_slot + j)
            for k in NEAR:
                send(rows, at_z(k), near_slot + k * NX + j)
        for k in far:
            rows = block_of(0, -k)
            arrived(array.at[:, rows], z_slot + k)
            for j in J_ORDER:
                send(rows, at_x(j), far_slot + k * NX + j)
        return z_slot, near_slot, far_slot

    def gather_wait(array, slots, chunk):
        z_slot, near_slot, far_slot = slots
        for offset in chunk:
            k = (NZ - offset) % NZ
            if k in NEAR:
                arrived(array.at[:, block_of(0, -k)], z_slot + k)
                for j in range(1, NX):
                    arrived(array.at[:, block_of(-j, -k)], near_slot + k * NX + j)
            elif k:
                for j in range(1, NX):
                    arrived(array.at[:, block_of(-j, -k)], far_slot + k * NX + j)

    def stacked(array, chunk):
        parts = [array[group(offset)] for offset in chunk]
        return parts[0] if len(parts) == 1 else jnp.concatenate(parts, axis=0)

    normed_slots = gather_start(normed, FAR)

    share_slot = fresh("recv", 5 * NY)
    both_slot = fresh("recv", NZ * NY)
    normed_x_slot, hidden_x_slot = fresh("recv"), fresh("recv")
    cot_x_slot, grad_x_slot = fresh("recv"), fresh("recv", NZ)
    raw_slot, out_slot, sum_slot = fresh("recv", NZ), fresh("recv", NZ * NX), fresh("recv", NZ)

    def up_step(n):
        chunk = FORWARD[n]
        size = len(chunk)
        gather_wait(normed, normed_slots, chunk)
        if n == 0:
            for copy in up_here:
                copy.wait()
            arrived(w_up.at[other], up_slot)
            arrived(w_ut.at[other], up_slot + 1)
        left, right = stacked(normed.at[0], chunk), stacked(normed.at[1], chunk)
        rows = pl.ds(0, size * GROUP)
        part_f[0, rows] = dot(left, w_up[0]) + dot(right, w_up[1])
        part_f[1, rows] = dot(left, w_ut[0]) + dot(right, w_ut[1])

        def share(j):
            mine = lax.rem(y + j, NY) * OWN
            return [part_f[:, pl.ds(pl.multiple_of(i * GROUP + mine, OWN), OWN)] for i in range(size)]

        for j in J_ORDER:
            for i, value in enumerate(share(j)):
                part_s[n, j - 1, i] = value.astype(bf16)
            few = pl.ds(0, size)
            copy_to(part_s.at[n, j - 1, few], part_r.at[n, j - 1, few], at_y(j), share_slot + n * NY + j)
        for i, value in enumerate(share(0)):
            part_own[n, i] = value
        if n == len(FORWARD) - 1:
            copy_to(normed.at[other], normed_x, sibling, normed_x_slot)

    def share_rows(offset, who):
        first = lax.rem(z + offset, NZ) * GROUP + lax.rem(who + NY, NY) * OWN
        return pl.ds(pl.multiple_of(first, OWN), OWN)

    def act_step(n):
        chunk = FORWARD[n]
        few = pl.ds(0, len(chunk))
        for j in range(1, NY):
            arrived(part_r.at[n, j - 1, few], share_slot + n * NY + j)
        for i, offset in enumerate(chunk):
            sums = part_own[n, i]
            for j in range(1, NY):
                sums = sums + part_r[n, j - 1, i].astype(f32)
            pre = sums[0] + up_bias[...].reshape(1, W)
            phi = 0.5 * (1.0 + lax.erf(pre * root_half))
            derivative = phi + pre * jnp.exp(-0.5 * pre * pre) * inv_root_two_pi
            rows = share_rows(offset, y)
            both[0, rows] = (pre * phi).astype(bf16)
            both[1, rows] = (derivative * sums[1]).astype(bf16)
            slope[offset] = derivative.astype(bf16)
            for j in J_ORDER:
                copy_to(both.at[:, rows], both.at[:, rows], at_y(j), both_slot + offset * NY + j)

    def down_step(n):
        chunk = FORWARD[n]
        for offset in chunk:
            for j in range(1, NY):
                arrived(both.at[:, share_rows(offset, y - j)], both_slot + offset * NY + j)
        if n == 0:
            for copy in down_here:
                copy.wait()
            arrived(w_dn.at[other], down_slot)
            arrived(w_dt.at[other], down_slot + 1)
        if n == len(FORWARD) - 1:
            copy_to(both.at[0], hidden_x, sibling, hidden_x_slot)
        hidden, hidden_tangent = stacked(both.at[0], chunk), stacked(both.at[1], chunk)
        rows = pl.ds(0, len(chunk) * GROUP)
        for f in range(2):
            out_f[0, f, rows] = dot(hidden, w_dn[f])
            out_f[1, f, rows] = dot(hidden_tangent, w_dn[f]) + dot(hidden, w_dt[f])
        for i, offset in enumerate(chunk):
            if offset in NEAR:
                raw_s[NEAR.index(offset)] = out_f[:, :, pl.ds(i * GROUP, GROUP)].astype(bf16)
                copy_to(raw_s.at[NEAR.index(offset)], raw_r.at[NEAR.index(offset)], at_z(offset), raw_slot + offset)
                continue
            if offset == 0:
                for k in NEAR:
                    arrived(raw_r.at[NEAR.index(k)], raw_slot + k)

            def part(j):
                first = pl.multiple_of(lax.rem(x + j, NX) * OWN, OWN)
                value = out_f[:, :, pl.ds(pl.multiple_of(first + i * GROUP, OWN), OWN)]
                if offset == 0:
                    for k in range(len(NEAR)):
                        value = value + raw_r[k, :, :, pl.ds(first, OWN)].astype(f32)
                return value

            for j in J_ORDER:
                out_s[offset, j - 1] = part(j).astype(bf16)
                copy_to(out_s.at[offset, j - 1], out_r.at[offset, j - 1], at_x(j), out_slot + offset * NX + j)
            own_x[offset] = part(0)

    def summed(offset):
        value = own_x[offset]
        for j in range(1, NX):
            arrived(out_r.at[offset, j - 1], out_slot + offset * NX + j)
            value = value + out_r[offset, j - 1].astype(f32)
        return value

    def sum_step(n):
        for offset in FORWARD[n]:
            sum_s[offset] = summed(offset).astype(bf16)
            copy_to(sum_s.at[offset], sum_r.at[offset], at_z(offset), sum_slot + offset)

    up_step(0)
    up_step(1)
    act_step(0)
    up_step(2)
    act_step(1)
    down_step(0)
    up_step(3)
    act_step(2)
    down_step(1)
    up_step(4)
    act_step(3)
    down_step(2)
    sum_step(1)
    act_step(4)
    down_step(3)
    sum_step(2)
    down_step(4)
    sum_step(3)

    arrived(curv.at[other], curv_slot)
    curv_here.wait()
    gain = by_half(gain_out, gout_x)
    factor = gain * gain * curv[...]
    outputs = summed(0)
    for k in FAR:
        arrived(sum_r.at[k], sum_slot + k)
        outputs = outputs + sum_r[k].astype(f32)

    output = tok[...].astype(f32) + outputs[0]
    tangent = outputs[1]
    total = row_sum(output)
    around = output - (total / (2 * W))[None]
    factor_around = factor * around
    stat_b[0] = columns([
        total, row_sum(around * around), row_sum(tangent), row_sum(around * tangent),
        row_sum(factor), row_sum(factor_around), row_sum(factor_around * around),
        row_sum(factor * tangent), row_sum(factor_around * tangent),
    ])
    stat_slot = fresh("recv", 3)
    for k in J_ORDER:
        copy_to(stat_b.at[0], stat_b.at[k], at_y(k), stat_slot + k - 1)
    for k in range(1, NY):
        arrived(stat_b.at[k], stat_slot + k - 1)
    stats = [[stat_b[k][:, i:i + 1] for i in range(9)] for k in range(NY)]
    center = (stats[0][0] + stats[1][0] + stats[2][0] + stats[3][0]) / D
    zero = jnp.zeros_like(center)
    square, sum_t, dot_t, f_0, f_1, f_2, ft_0, ft_1 = (zero,) * 8
    for s in stats:
        off = s[0] / (2 * W) - center
        square = square + s[1] + (2 * W) * (off * off)
        sum_t = sum_t + s[2]
        dot_t = dot_t + s[3] + off * s[2]
        f_0 = f_0 + s[4]
        f_1 = f_1 + s[5] + off * s[4]
        f_2 = f_2 + s[6] + 2.0 * off * s[5] + off * off * s[4]
        ft_0 = ft_0 + s[7]
        ft_1 = ft_1 + s[8] + off * s[7]
    inverse = lax.rsqrt(square / D + epsilon)
    mean_t = sum_t / D
    mean_nt = dot_t * inverse / D
    fn_1 = f_1 * inverse
    mean_w = (ft_0 - mean_t * f_0 - mean_nt * fn_1) * inverse / D
    mean_nw = (ft_1 * inverse - mean_t * fn_1 - mean_nt * (f_2 * inverse * inverse)) * inverse / D
    normal = (output - center[None]) * inverse[None]
    weighted = factor * ((tangent - mean_t[None] - normal * mean_nt[None]) * inverse[None])
    cot[:, block] = ((weighted - mean_w[None] - normal * mean_nw[None]) * inverse[None]).astype(bf16)

    cot_slots = gather_start(cot, FAR[::-1])
    back_slot = fresh("recv", 5 * NY)
    grad_slot = fresh("recv", NZ * NY)

    def back_step(n):
        chunk = BACKWARD[n]
        size = len(chunk)
        gather_wait(cot, cot_slots, chunk)
        left, right = stacked(cot.at[0], chunk), stacked(cot.at[1], chunk)
        back_f[pl.ds(0, size * GROUP)] = dot_last(left, w_dn[0]) + dot_last(right, w_dn[1])

        def share(j):
            mine = lax.rem(y + j, NY) * OWN
            return [back_f[pl.ds(pl.multiple_of(i * GROUP + mine, OWN), OWN)] for i in range(size)]

        for j in J_ORDER:
            for i, value in enumerate(share(j)):
                back_s[n, j - 1, i] = value.astype(bf16)
            few = pl.ds(0, size)
            copy_to(back_s.at[n, j - 1, few], back_r.at[n, j - 1, few], at_y(j), back_slot + n * NY + j)
        for i, value in enumerate(share(0)):
            back_own[n, i] = value
        if n == len(BACKWARD) - 1:
            copy_to(cot.at[other], cot_x, sibling, cot_x_slot)

    def grad_step(n):
        chunk = BACKWARD[n]
        few = pl.ds(0, len(chunk))
        for j in range(1, NY):
            arrived(back_r.at[n, j - 1, few], back_slot + n * NY + j)
        for i, offset in enumerate(chunk):
            sums = back_own[n, i]
            for j in range(1, NY):
                sums = sums + back_r[n, j - 1, i].astype(f32)
            rows = share_rows(offset, y)
            grad[rows] = (sums * slope[offset].astype(f32)).astype(bf16)
            for j in J_ORDER:
                copy_to(grad.at[rows], grad.at[rows], at_y(j), grad_slot + offset * NY + j)

    def swap_step(n):
        for offset in BACKWARD[n]:
            for j in range(1, NY):
                arrived(grad.at[share_rows(offset, y - j)], grad_slot + offset * NY + j)
            rows = group(offset)
            copy_to(grad.at[rows], grad_x.at[rows], sibling, grad_x_slot + offset)

    def product(first, first_x, second, second_x, result, slot):
        copies = []
        for n in range(TILES):
            part = pl.ds(n * TILE, TILE)
            stage[slot, part] = dot_first(first(part), second[...]) + dot_first(first_x(part), second_x[...])
            copies.append(copy_here(stage.at[slot, part], result.at[part]))
        return copies

    back_step(0)
    back_step(1)
    back_step(2)
    grad_step(0)
    back_step(3)
    grad_step(1)
    swap_step(0)
    back_step(4)
    grad_step(2)
    swap_step(1)
    grad_step(3)
    arrived(hidden_x, hidden_x_slot)
    arrived(normed_x, normed_x_slot)
    arrived(cot_x, cot_x_slot)
    grad_step(4)
    written = product(
        lambda part: both[0, :, part], lambda part: hidden_x[:, part], cot.at[c], cot_x, down_out, 0,
    )
    swap_step(2)
    swap_step(3)
    swap_step(4)
    for k in range(NZ):
        arrived(grad_x.at[group(k)], grad_x_slot + k)
    written += product(
        lambda part: normed[c, :, part], lambda part: normed_x[:, part], grad, grad_x, up_out, 1,
    )
    for copy in written:
        copy.wait()
    for copy in sends:
        copy.wait_send()
    assert counts["send"] <= N_SEND and counts["recv"] <= N_RECV and counts["local"] <= N_LOCAL


def on_device(*args):
    any_ = pl.BlockSpec(memory_space=pl.ANY)
    vmem = pl.BlockSpec(memory_space=pltpu.VMEM)
    scratch = [
        ((2, W, W), bf16), ((2, W, W), bf16), ((2, W, W), bf16), ((2, W, W), bf16),
        ((2, OWN, W), bf16), ((2, OWN, W), f32), ((W,), f32), ((W,), f32), ((W,), f32),
        ((NY, OWN, 128), f32), ((NY, OWN, 128), f32),
        ((2, ROWS, W), bf16), ((ROWS, W), bf16),
        ((2, 2 * GROUP, W), f32), ((5, 3, 2, 2, OWN, W), bf16), ((5, 3, 2, 2, OWN, W), bf16), ((5, 2, 2, OWN, W), f32),
        ((2, ROWS, W), bf16), ((ROWS, W), bf16), ((NZ, OWN, W), bf16),
        ((2, 2, 2 * GROUP, W), f32), ((2, 2, 2, GROUP, W), bf16), ((2, 2, 2, GROUP, W), bf16),
        ((7, 2, 2, OWN, W), f32), ((7, 3, 2, 2, OWN, W), bf16), ((7, 3, 2, 2, OWN, W), bf16),
        ((7, 2, 2, OWN, W), bf16), ((7, 2, 2, OWN, W), bf16),
        ((2, ROWS, W), bf16), ((ROWS, W), bf16),
        ((2 * GROUP, W), f32), ((5, 3, 2, OWN, W), bf16), ((5, 3, 2, OWN, W), bf16), ((5, 2, OWN, W), f32),
        ((ROWS, W), bf16), ((ROWS, W), bf16), ((2, W, W), f32),
    ]
    return pl.pallas_call(
        kernel,
        out_shape=(jax.ShapeDtypeStruct((W, W), f32), jax.ShapeDtypeStruct((W, W), f32)),
        in_specs=[any_, vmem, vmem, any_, vmem, any_, vmem, any_, any_, any_],
        out_specs=(any_, any_),
        scratch_shapes=[pltpu.VMEM(shape, dtype) for shape, dtype in scratch]
        + [pltpu.SemaphoreType.DMA((N_SEND,)), pltpu.SemaphoreType.DMA((N_RECV,)), pltpu.SemaphoreType.DMA((N_LOCAL,))],
        compiler_params=pltpu.CompilerParams(
            collective_id=0, has_side_effects=True, vmem_limit_bytes=60 * 2**20
        ),
        cost_estimate=pl.CostEstimate(flops=9663676416, bytes_accessed=9437184, transcendentals=262144),
        name="gauss_newton",
    )(*args)


def solution(mesh):
    return jax.shard_map(
        on_device,
        mesh=mesh,
        in_specs=(
            P("dp", "tensor"),
            P("tensor"),
            P("tensor"),
            P("tensor", "dp"),
            P("dp"),
            P("dp", "tensor"),
            P("tensor"),
            P("dp", "tensor"),
            P("tensor", "dp"),
            P("dp", "tensor"),
        ),
        out_specs=(P("tensor", "dp"), P("dp", "tensor")),
        check_vma=False,
    )
```

```python
import functools

import jax
import jax.numpy as jnp
from jax import lax
from jax.experimental import pallas as pl
from jax.experimental.pallas import tpu as pltpu
from jax.sharding import PartitionSpec as P

D = 6144
epsilon = 1e-05
root_half = 0.7071067811865476
inv_root_two_pi = 0.3989422804014327

f32 = jnp.float32
bf16 = jnp.bfloat16
MESH = pl.DeviceIdType.MESH

NX, NZ, NY = 4, 8, 4
OWN = 16
GROUP = NX * OWN
ROWS = NZ * GROUP
W = 768
TILE = 256
TILES = W // TILE
FORWARD = {"0": (0,), "4": (4,), "17": (1, 7), "3": (3,), "5": (5,), "2": (2,), "6": (6,)}
BACKWARD = {"0": (0,), "17": (1, 7), "26": (2, 6), "35": (3, 5), "4": (4,)}
NEAR = (1, 7)
FAR = (4, 3, 5, 2, 6)
J_ORDER = (2, 1, 3)

N_SEND = 22
N_RECV = 94
N_LOCAL = 11


def dot(a, b):
    return jnp.dot(a, b, preferred_element_type=f32)


def dot_last(a, b):
    return lax.dot_general(a, b, (((1,), (1,)), ((), ())), preferred_element_type=f32)


def dot_first(a, b):
    return lax.dot_general(a, b, (((0,), (0,)), ((), ())), preferred_element_type=f32)


def columns(values):
    lane = lax.broadcasted_iota(jnp.int32, (OWN, 128), 1)
    out = jnp.zeros((OWN, 128), f32)
    for at, value in enumerate(values):
        out = jnp.where(lane == at, value, out)
    return out


def row_sum(pair):
    return jnp.sum(pair[0] + pair[1], axis=1, keepdims=True)


def kernel(
    tokens, gain_in, shift_in, up_weight, up_bias, down_weight, gain_out, curvature, up_tangent, down_tangent,
    down_out, normed_out, normed_x_out, grad_out, grad_x_out,
    w_up, w_ut, w_dn, w_dt, tok, curv, gin_x, sin_x, gout_x,
    stat_a, stat_b, normed, part_f, part_s, part_r, part_own,
    both, hidden_x, slope, out_f, raw_s, raw_r, own_x, out_s, out_r, sum_s, sum_r,
    cot, cot_x, back_f, back_s, back_r, back_own, grad, stage, w_dn_t,
    send_sem, recv_sem, local_sem,
):
    d, t = lax.axis_index("dp"), lax.axis_index("tensor")
    x, z = d // NZ, lax.rem(d, NZ)
    y, c = t // 2, lax.rem(t, 2)
    other = 1 - c

    def at_x(k):
        return (lax.rem(x + k, NX) * NZ + z, t)

    def at_z(k):
        return (x * NZ + lax.rem(z + k, NZ), t)

    def at_y(k):
        return (d, lax.rem(y + k, NY) * 2 + c)

    sibling = (d, y * 2 + other)
    ends, counts = [], {"send": 0, "recv": 0, "local": 0}

    def fresh(kind, n=1):
        at = counts[kind]
        counts[kind] += n
        return at

    def sends_of(ref):
        slot = fresh("send")
        ends.append((ref, slot))
        return slot

    def copy_to(src, dst, device, sent, slot):
        pltpu.make_async_remote_copy(
            src_ref=src, dst_ref=dst, send_sem=send_sem.at[sent],
            recv_sem=recv_sem.at[slot], device_id=device, device_id_type=MESH,
        ).start()

    def bytes_of(ref, sent, slot):
        return pltpu.make_async_remote_copy(
            src_ref=ref, dst_ref=ref, send_sem=send_sem.at[sent],
            recv_sem=recv_sem.at[slot], device_id=sibling, device_id_type=MESH,
        )

    def arrived(ref, slot):
        bytes_of(ref, 0, slot).wait_recv()

    def copy_here(src, dst):
        copy = pltpu.make_async_copy(src, dst, local_sem.at[fresh("local")])
        copy.start()
        return copy

    own_rows = pl.ds(pl.multiple_of(c * OWN, OWN), OWN)
    their_rows = pl.ds(pl.multiple_of(other * OWN, OWN), OWN)
    tok_here = copy_here(tokens.at[own_rows], tok.at[c])
    curv_here = copy_here(curvature.at[own_rows], curv.at[c])
    up_here = [copy_here(up_weight, w_up.at[c]), copy_here(up_tangent, w_ut.at[c])]
    down_here = [copy_here(down_weight, w_dn.at[c]), copy_here(down_tangent, w_dt.at[c])]
    barrier = pltpu.get_barrier_semaphore()
    peers = [sibling] + [at_x(k) for k in range(1, NX)] + [at_z(k) for k in range(1, NZ)] + [at_y(k) for k in range(1, NY)]
    for peer in peers:
        pl.semaphore_signal(barrier, inc=1, device_id=peer, device_id_type=MESH)
    pl.semaphore_wait(barrier, len(peers))

    tok_slot, params_slot, curv_slot = fresh("recv"), fresh("recv", 3), fresh("recv")
    up_slot, down_slot = fresh("recv"), fresh("recv")
    copy_to(tokens.at[their_rows], tok.at[c], sibling, sends_of(tok.at[c]), tok_slot)
    for i, (mine, theirs) in enumerate(((gain_in, gin_x), (shift_in, sin_x), (gain_out, gout_x))):
        copy_to(mine, theirs, sibling, sends_of(theirs), params_slot + i)

    def send_weights(pairs, whole, slot):
        sent = sends_of(whole)
        for mine, theirs in pairs:
            copy_to(mine, theirs.at[c], sibling, sent, slot)

    tok_here.wait()
    arrived(tok.at[other], tok_slot)
    source = tok[...].astype(f32)
    total = row_sum(source)
    spread = source - (total / (2 * W))[None]
    stat_a[0] = columns([total, row_sum(spread * spread)])
    stat_slot, sent = fresh("recv"), sends_of(stat_a.at[pl.ds(1, 3)])
    for k in J_ORDER:
        copy_to(stat_a.at[0], stat_a.at[k], at_y(k), sent, stat_slot)
    arrived(gin_x, params_slot)
    arrived(sin_x, params_slot + 1)
    arrived(gout_x, params_slot + 2)

    def by_half(mine, theirs):
        mine, theirs = mine[...].reshape(1, W), theirs[...].reshape(1, W)
        first = jnp.where(c == 0, mine, theirs)
        second = jnp.where(c == 0, theirs, mine)
        return jnp.stack([first, second])

    gain, shift = by_half(gain_in, gin_x), by_half(shift_in, sin_x)
    arrived(stat_a.at[pl.ds(1, 3)], stat_slot)
    totals = [stat_a[k][:, 0:1] for k in range(NY)]
    center = (totals[0] + totals[1] + totals[2] + totals[3]) / D
    variance = jnp.zeros_like(center)
    for k in range(NY):
        off = totals[k] / (2 * W) - center
        variance = variance + stat_a[k][:, 1:2] + (2 * W) * (off * off)
    inverse = lax.rsqrt(variance / D + epsilon)
    def group(k):
        return pl.ds(pl.multiple_of(lax.rem(z + NZ + k, NZ) * GROUP, GROUP), GROUP)

    def block_of(j, k):
        first = lax.rem(z + NZ + k, NZ) * GROUP + lax.rem(x + NX + j, NX) * OWN
        return pl.ds(pl.multiple_of(first, OWN), OWN)

    block = block_of(0, 0)
    normed[:, block] = ((source - center[None]) * inverse[None] * gain + shift).astype(bf16)

    def three_of(offset):
        first = lax.rem(z + NZ + offset, NZ) * GROUP
        return pl.ds(pl.multiple_of(first, GROUP), GROUP - OWN)

    def gather_start(array, far, between):
        sent = sends_of(array.at[:, pl.ds(0, ROWS - OWN)])

        def send(rows, device, slot):
            copy_to(array.at[:, rows], array.at[:, rows], device, sent, slot)

        z_slot, x_slot, last_slot = fresh("recv", NZ), fresh("recv", NX), fresh("recv", NZ)
        for j in J_ORDER:
            send(block, at_x(j), x_slot + j)
        for k in NEAR + far:
            send(block, at_z(k), last_slot + k if k in NEAR else z_slot + k)
        between()
        for j in (1, 3, 2):
            rows = block_of(-j, 0)
            arrived(array.at[:, rows], x_slot + j)
            for k in NEAR:
                send(rows, at_z(k), last_slot + k)
        for k in far:
            rows = block_of(0, -k)
            arrived(array.at[:, rows], z_slot + k)
            for j in J_ORDER:
                send(rows, at_x(j), last_slot + k)
        return last_slot

    def gather_wait(array, last_slot, chunk):
        for offset in chunk:
            k = (NZ - offset) % NZ
            if k in NEAR:
                arrived(array.at[:, group(-k)], last_slot + k)
            elif k:
                arrived(array.at[:, three_of(-k)], last_slot + k)

    def stacked(array, chunk):
        parts = [array[group(offset)] for offset in chunk]
        return parts[0] if len(parts) == 1 else jnp.concatenate(parts, axis=0)

    normed_slots = gather_start(
        normed, (3, 5, 4, 2, 6), lambda: send_weights(((up_weight, w_up), (up_tangent, w_ut)), w_up, up_slot)
    )
    send_weights(((down_weight, w_dn), (down_tangent, w_dt)), w_dn, down_slot)
    copy_to(curvature.at[their_rows], curv.at[c], sibling, sends_of(curv.at[c]), curv_slot)

    share_slot, share_sent = fresh("recv", NZ), sends_of(part_s)
    both_slot, both_sent = fresh("recv", NZ), sends_of(both.at[:, pl.ds(0, ROWS - NZ * OWN)])
    normed_x_slot, hidden_x_slot = fresh("recv"), fresh("recv")
    raw_slot, raw_sent = fresh("recv", 2), sends_of(raw_s)
    out_slot, out_sent = fresh("recv", 6), sends_of(out_s)
    sum_slot, sum_sent = fresh("recv"), sends_of(sum_s)
    ordered = (0,) + FAR

    def up_step(name):
        chunk = FORWARD[name]
        size = len(chunk)
        gather_wait(normed, normed_slots, chunk)
        if name == "0":
            for copy in up_here:
                copy.wait()
            arrived(w_up, up_slot)
        left, right = stacked(normed.at[0], chunk), stacked(normed.at[1], chunk)
        rows = pl.ds(0, size * GROUP)
        part_f[0, rows] = dot(left, w_up[0]) + dot(right, w_up[1])
        part_f[1, rows] = dot(left, w_ut[0]) + dot(right, w_ut[1])

        def share(i, j):
            mine = lax.rem(y + j, NY) * OWN
            return part_f[:, pl.ds(pl.multiple_of(i * GROUP + mine, OWN), OWN)]

        for j in J_ORDER:
            for i, offset in enumerate(chunk):
                part_s[offset, j - 1] = share(i, j).astype(bf16)
                copy_to(part_s.at[offset, j - 1], part_r.at[offset, j - 1], at_y(j), share_sent, share_slot + offset)
        for i, offset in enumerate(chunk):
            part_own[offset] = share(i, 0)

    def share_rows(offset, who):
        first = lax.rem(z + offset, NZ) * GROUP + lax.rem(who + NY, NY) * OWN
        return pl.ds(pl.multiple_of(first, OWN), OWN)

    def act_step(name):
        for offset in FORWARD[name]:
            arrived(part_r.at[offset], share_slot + offset)
            sums = part_own[offset]
            for j in range(1, NY):
                sums = sums + part_r[offset, j - 1].astype(f32)
            pre = sums[0] + up_bias[...].reshape(1, W)
            phi = 0.5 * (1.0 + lax.erf(pre * root_half))
            derivative = phi + pre * jnp.exp(-0.5 * pre * pre) * inv_root_two_pi
            rows = share_rows(offset, y)
            both[0, rows] = (pre * phi).astype(bf16)
            both[1, rows] = (derivative * sums[1]).astype(bf16)
            slope[offset] = derivative.astype(bf16)
            for j in J_ORDER:
                copy_to(both.at[:, rows], both.at[:, rows], at_y(j), both_sent, both_slot + offset)

    def down_step(name):
        chunk = FORWARD[name]
        for offset in chunk:
            arrived(both.at[:, three_of(offset)], both_slot + offset)
        if name == "4":
            for copy in down_here:
                copy.wait()
            arrived(w_dn, down_slot)
        hidden, hidden_tangent = stacked(both.at[0], chunk), stacked(both.at[1], chunk)
        rows = pl.ds(0, len(chunk) * GROUP)
        for f in range(2):
            out_f[0, f, rows] = dot(hidden, w_dn[f])
            out_f[1, f, rows] = dot(hidden_tangent, w_dn[f]) + dot(hidden, w_dt[f])
        for i, offset in enumerate(chunk):
            if offset in NEAR:
                at = NEAR.index(offset)
                raw_s[at] = out_f[:, :, pl.ds(i * GROUP, GROUP)].astype(bf16)
                copy_to(raw_s.at[at], raw_r.at[at], at_z(offset), raw_sent, raw_slot + at)
                continue
            at = ordered.index(offset)
            if offset == 0:
                for k in range(len(NEAR)):
                    arrived(raw_r.at[k], raw_slot + k)

            def part(j):
                first = pl.multiple_of(lax.rem(x + j, NX) * OWN, OWN)
                value = out_f[:, :, pl.ds(first, OWN)]
                if offset == 0:
                    for k in range(len(NEAR)):
                        value = value + raw_r[k, :, :, pl.ds(first, OWN)].astype(f32)
                return value

            for j in J_ORDER:
                out_s[at, j - 1] = part(j).astype(bf16)
                copy_to(out_s.at[at, j - 1], out_r.at[at, j - 1], at_x(j), out_sent, out_slot + at)
            own_x[at] = part(0)

    def summed(offset):
        at = ordered.index(offset)
        arrived(out_r.at[at], out_slot + at)
        value = own_x[at]
        for j in range(1, NX):
            value = value + out_r[at, j - 1].astype(f32)
        return value

    def sum_step(name):
        for offset in FORWARD[name]:
            at = FAR.index(offset)
            sum_s[at] = summed(offset).astype(bf16)
            copy_to(sum_s.at[at], sum_r.at[at], at_z(offset), sum_sent, sum_slot)

    steps = {"u": up_step, "a": act_step, "d": down_step, "s": sum_step}
    order = ("u0", "u17", "u5", "u4", "u3", "u6", "a4", "a3", "a6", "a17", "d4", "u2", "d3", "a5", "d6", "d17", "a2", "s4", "d5", "a0", "s3", "d2", "s5", "d0", "s6", "s2")
    for step in order:
        if step == "a2":
            copy_to(normed.at[other], normed_x_out, sibling, sends_of(normed.at[other]), normed_x_slot)
            normed_written = copy_here(normed.at[c], normed_out)
            for f in range(2):
                w_dn_t[f] = w_dn[f].T
        steps[step[0]](step[1:])
    copy_to(both.at[0], hidden_x, sibling, sends_of(both.at[0]), hidden_x_slot)

    arrived(curv.at[other], curv_slot)
    curv_here.wait()
    gain = by_half(gain_out, gout_x)
    factor = gain * gain * curv[...]
    outputs = summed(0)
    arrived(sum_r, sum_slot)
    for k in range(len(FAR)):
        outputs = outputs + sum_r[k].astype(f32)

    output = tok[...].astype(f32) + outputs[0]
    tangent = outputs[1]
    total = row_sum(output)
    around = output - (total / (2 * W))[None]
    factor_around = factor * around
    stat_b[0] = columns([
        total, row_sum(around * around), row_sum(tangent), row_sum(around * tangent),
        row_sum(factor), row_sum(factor_around), row_sum(factor_around * around),
        row_sum(factor * tangent), row_sum(factor_around * tangent),
    ])
    stat_slot, sent = fresh("recv"), sends_of(stat_b.at[pl.ds(1, 3)])
    for k in J_ORDER:
        copy_to(stat_b.at[0], stat_b.at[k], at_y(k), sent, stat_slot)
    arrived(stat_b.at[pl.ds(1, 3)], stat_slot)
    stats = [[stat_b[k][:, i:i + 1] for i in range(9)] for k in range(NY)]
    center = (stats[0][0] + stats[1][0] + stats[2][0] + stats[3][0]) / D
    zero = jnp.zeros_like(center)
    square, sum_t, dot_t, f_0, f_1, f_2, ft_0, ft_1 = (zero,) * 8
    for s in stats:
        off = s[0] / (2 * W) - center
        square = square + s[1] + (2 * W) * (off * off)
        sum_t = sum_t + s[2]
        dot_t = dot_t + s[3] + off * s[2]
        f_0 = f_0 + s[4]
        f_1 = f_1 + s[5] + off * s[4]
        f_2 = f_2 + s[6] + 2.0 * off * s[5] + off * off * s[4]
        ft_0 = ft_0 + s[7]
        ft_1 = ft_1 + s[8] + off * s[7]
    inverse = lax.rsqrt(square / D + epsilon)
    mean_t = sum_t / D
    mean_nt = dot_t * inverse / D
    fn_1 = f_1 * inverse
    mean_w = (ft_0 - mean_t * f_0 - mean_nt * fn_1) * inverse / D
    mean_nw = (ft_1 * inverse - mean_t * fn_1 - mean_nt * (f_2 * inverse * inverse)) * inverse / D
    normal = (output - center[None]) * inverse[None]
    weighted = factor * ((tangent - mean_t[None] - normal * mean_nt[None]) * inverse[None])
    cot[:, block] = ((weighted - mean_w[None] - normal * mean_nw[None]) * inverse[None]).astype(bf16)

    cot_slots = gather_start(cot, FAR[::-1], lambda: None)
    back_slot, back_sent = fresh("recv", NZ), sends_of(back_s)
    grad_slot, grad_sent = fresh("recv", NZ), sends_of(grad.at[pl.ds(0, ROWS - NZ * OWN)])
    cot_x_slot, cot_x_sent = fresh("recv"), sends_of(cot.at[other])
    grad_x_slot, grad_x_sent = fresh("recv"), sends_of(grad)
    grad_written = fresh("local")

    def back_step(name):
        chunk = BACKWARD[name]
        size = len(chunk)
        gather_wait(cot, cot_slots, chunk)
        left, right = stacked(cot.at[0], chunk), stacked(cot.at[1], chunk)
        back_f[pl.ds(0, size * GROUP)] = dot(left, w_dn_t[0]) + dot(right, w_dn_t[1])

        def share(i, j):
            mine = lax.rem(y + j, NY) * OWN
            return back_f[pl.ds(pl.multiple_of(i * GROUP + mine, OWN), OWN)]

        for j in J_ORDER:
            for i, offset in enumerate(chunk):
                back_s[offset, j - 1] = share(i, j).astype(bf16)
                copy_to(back_s.at[offset, j - 1], back_r.at[offset, j - 1], at_y(j), back_sent, back_slot + offset)
        for i, offset in enumerate(chunk):
            back_own[offset] = share(i, 0)
            rows = group(offset)
            copy_to(cot.at[other, rows], cot_x.at[rows], sibling, cot_x_sent, cot_x_slot)

    def grad_step(name):
        for offset in BACKWARD[name]:
            arrived(back_r.at[offset], back_slot + offset)
            sums = back_own[offset]
            for j in range(1, NY):
                sums = sums + back_r[offset, j - 1].astype(f32)
            rows = share_rows(offset, y)
            grad[rows] = (sums * slope[offset].astype(f32)).astype(bf16)
            for j in J_ORDER:
                copy_to(grad.at[rows], grad.at[rows], at_y(j), grad_sent, grad_slot + offset)

    def swap_step(name):
        for offset in BACKWARD[name]:
            arrived(grad.at[three_of(offset)], grad_slot + offset)
            rows = group(offset)
            copy_to(grad.at[rows], grad_x_out.at[rows], sibling, grad_x_sent, grad_x_slot)
            copy = pltpu.make_async_copy(grad.at[rows], grad_out.at[rows], local_sem.at[grad_written])
            copy.start()

    steps = {"b": back_step, "g": grad_step, "w": swap_step}
    for step in ("b0", "b17", "g0", "b26", "g17", "b35", "b4", "g26", "g35", "g4", "w0", "w17", "w26"):
        steps[step[0]](step[1:])
    arrived(hidden_x, hidden_x_slot)
    arrived(cot_x, cot_x_slot)
    written = [normed_written]
    for n in range(TILES):
        part = pl.ds(n * TILE, TILE)
        stage[part] = dot_first(both[0, :, part], cot[c]) + dot_first(hidden_x[:, part], cot_x[...])
        written.append(copy_here(stage.at[part], down_out.at[part]))
    swap_step("35")
    swap_step("4")
    arrived(normed_x_out, normed_x_slot)
    for copy in written:
        copy.wait()
    for ref, slot in ends:
        bytes_of(ref, slot, 0).wait_send()
    pltpu.make_async_copy(grad, grad_out, local_sem.at[grad_written]).wait()
    arrived(grad_x_out, grad_x_slot)
    assert counts["send"] <= N_SEND and counts["recv"] <= N_RECV and counts["local"] <= N_LOCAL


def finish_kernel(down, normed, normed_x, grad, grad_x, up_out, down_out, n_own, n_x, g_own, g_x, moving, stage, sems):
    pairs = ((normed, n_own), (grad, g_own), (normed_x, n_x), (grad_x, g_x), (down, moving))
    loads = [pltpu.make_async_copy(src, dst, sems.at[i]) for i, (src, dst) in enumerate(pairs)]
    for copy in loads:
        copy.start()
    for copy in loads[:2]:
        copy.wait()
    for n in range(TILES):
        part = pl.ds(n * TILE, TILE)
        stage[part] = dot_first(n_own[:, part], g_own[...])
    for copy in loads[2:]:
        copy.wait()
    moved = pltpu.make_async_copy(moving, down_out, sems.at[0])
    moved.start()
    written = [moved]
    for n in range(TILES):
        part = pl.ds(n * TILE, TILE)
        stage[part] += dot_first(n_x[:, part], g_x[...])
        copy = pltpu.make_async_copy(stage.at[part], up_out.at[part], sems.at[5 + n])
        copy.start()
        written.append(copy)
    for copy in written:
        copy.wait()


def on_device(*args):
    any_ = pl.BlockSpec(memory_space=pl.ANY)
    vmem = pl.BlockSpec(memory_space=pltpu.VMEM)
    scratch = [
        ((2, W, W), bf16), ((2, W, W), bf16), ((2, W, W), bf16), ((2, W, W), bf16),
        ((2, OWN, W), bf16), ((2, OWN, W), f32), ((W,), f32), ((W,), f32), ((W,), f32),
        ((NY, OWN, 128), f32), ((NY, OWN, 128), f32),
        ((2, ROWS, W), bf16),
        ((2, 2 * GROUP, W), f32), ((NZ, 3, 2, OWN, W), bf16), ((NZ, 3, 2, OWN, W), bf16), ((NZ, 2, OWN, W), f32),
        ((2, ROWS, W), bf16), ((ROWS, W), bf16), ((NZ, OWN, W), bf16),
        ((2, 2, 2 * GROUP, W), f32), ((2, 2, 2, GROUP, W), bf16), ((2, 2, 2, GROUP, W), bf16),
        ((6, 2, 2, OWN, W), f32), ((6, 3, 2, 2, OWN, W), bf16), ((6, 3, 2, 2, OWN, W), bf16),
        ((5, 2, 2, OWN, W), bf16), ((5, 2, 2, OWN, W), bf16),
        ((2, ROWS, W), bf16), ((ROWS, W), bf16),
        ((2 * GROUP, W), f32), ((NZ, 3, OWN, W), bf16), ((NZ, 3, OWN, W), bf16), ((NZ, OWN, W), f32),
        ((ROWS, W), bf16), ((W, W), f32), ((2, W, W), bf16),
    ]
    product = jax.ShapeDtypeStruct((W, W), f32)
    rows = jax.ShapeDtypeStruct((ROWS, W), bf16)
    partial = pl.pallas_call(
        kernel,
        out_shape=(product, rows, rows, rows, rows),
        in_specs=[any_, vmem, vmem, any_, vmem, any_, vmem, any_, any_, any_],
        out_specs=(any_,) * 5,
        scratch_shapes=[pltpu.VMEM(shape, dtype) for shape, dtype in scratch]
        + [pltpu.SemaphoreType.DMA((N_SEND,)), pltpu.SemaphoreType.DMA((N_RECV,)), pltpu.SemaphoreType.DMA((N_LOCAL,))],
        compiler_params=pltpu.CompilerParams(
            collective_id=0, has_side_effects=True, vmem_limit_bytes=60 * 2**20
        ),
        cost_estimate=pl.CostEstimate(flops=9663676416, bytes_accessed=9437184, transcendentals=262144),
        name="gauss_newton",
    )(*args)
    return pl.pallas_call(
        finish_kernel,
        out_shape=(product, product),
        in_specs=[any_] * 5,
        out_specs=(any_, any_),
        scratch_shapes=[pltpu.VMEM((ROWS, W), bf16)] * 4
        + [pltpu.VMEM((W, W), f32)] * 2
        + [pltpu.SemaphoreType.DMA((8,))],
        compiler_params=pltpu.CompilerParams(vmem_limit_bytes=60 * 2**20),
        cost_estimate=pl.CostEstimate(flops=1207959552, bytes_accessed=10223616, transcendentals=0),
        name="finish",
    )(*partial)


def solution(mesh):
    return jax.shard_map(
        on_device,
        mesh=mesh,
        in_specs=(
            P("dp", "tensor"),
            P("tensor"),
            P("tensor"),
            P("tensor", "dp"),
            P("dp"),
            P("dp", "tensor"),
            P("tensor"),
            P("dp", "tensor"),
            P("tensor", "dp"),
            P("dp", "tensor"),
        ),
        out_specs=(P("tensor", "dp"), P("dp", "tensor")),
        check_vma=False,
    )
```

```python
import functools

import jax
import jax.numpy as jnp
from jax import lax
from jax.experimental import pallas as pl
from jax.experimental.pallas import tpu as pltpu
from jax.sharding import PartitionSpec as P

D = 6144
epsilon = 1e-05
root_half = 0.7071067811865476
inv_root_two_pi = 0.3989422804014327

f32 = jnp.float32
bf16 = jnp.bfloat16
MESH = pl.DeviceIdType.MESH

NX, NZ, NY = 4, 8, 4
OWN = 16
GROUP = NX * OWN
ROWS = NZ * GROUP
W = 768
TILE = 256
TILES = W // TILE
FORWARD = {"0": (0,), "4": (4,), "17": (1, 7), "3": (3,), "5": (5,), "2": (2,), "6": (6,)}
BACKWARD = {"0": (0,), "17": (1, 7), "26": (2, 6), "35": (3, 5), "4": (4,)}
NEAR = (1, 7)
FAR = (4, 3, 5, 2, 6)
J_ORDER = (2, 1, 3)

N_SEND = 22
N_RECV = 94
N_LOCAL = 11


def dot(a, b):
    return jnp.dot(a, b, preferred_element_type=f32)


def dot_last(a, b):
    return lax.dot_general(a, b, (((1,), (1,)), ((), ())), preferred_element_type=f32)


def dot_first(a, b):
    return lax.dot_general(a, b, (((0,), (0,)), ((), ())), preferred_element_type=f32)


def columns(values):
    lane = lax.broadcasted_iota(jnp.int32, (OWN, 128), 1)
    out = jnp.zeros((OWN, 128), f32)
    for at, value in enumerate(values):
        out = jnp.where(lane == at, value, out)
    return out


def row_sum(pair):
    return jnp.sum(pair[0] + pair[1], axis=1, keepdims=True)


def kernel(
    tokens, gain_in, shift_in, up_weight, up_bias, down_weight, gain_out, curvature, up_tangent, down_tangent,
    down_out, normed_out, normed_x_out, grad_out, grad_x_out,
    w_up, w_ut, w_dn, w_dt, tok, curv, gin_x, sin_x, gout_x,
    stat_a, stat_b, normed, part_f, part_s, part_r, part_own,
    both, hidden_x, slope, out_f, raw_s, raw_r, own_x, out_s, out_r, sum_s, sum_r,
    cot, cot_x, back_f, back_s, back_r, back_own, grad, stage, w_dn_t,
    send_sem, recv_sem, local_sem,
):
    d, t = lax.axis_index("dp"), lax.axis_index("tensor")
    x, z = d // NZ, lax.rem(d, NZ)
    y, c = t // 2, lax.rem(t, 2)
    other = 1 - c

    def at_x(k):
        return (lax.rem(x + k, NX) * NZ + z, t)

    def at_z(k):
        return (x * NZ + lax.rem(z + k, NZ), t)

    def at_y(k):
        return (d, lax.rem(y + k, NY) * 2 + c)

    sibling = (d, y * 2 + other)
    ends, counts = [], {"send": 0, "recv": 0, "local": 0}

    def fresh(kind, n=1):
        at = counts[kind]
        counts[kind] += n
        return at

    def sends_of(ref):
        slot = fresh("send")
        ends.append((ref, slot))
        return slot

    def copy_to(src, dst, device, sent, slot):
        pltpu.make_async_remote_copy(
            src_ref=src, dst_ref=dst, send_sem=send_sem.at[sent],
            recv_sem=recv_sem.at[slot], device_id=device, device_id_type=MESH,
        ).start()

    def bytes_of(ref, sent, slot):
        return pltpu.make_async_remote_copy(
            src_ref=ref, dst_ref=ref, send_sem=send_sem.at[sent],
            recv_sem=recv_sem.at[slot], device_id=sibling, device_id_type=MESH,
        )

    def arrived(ref, slot):
        bytes_of(ref, 0, slot).wait_recv()

    def copy_here(src, dst):
        copy = pltpu.make_async_copy(src, dst, local_sem.at[fresh("local")])
        copy.start()
        return copy

    own_rows = pl.ds(pl.multiple_of(c * OWN, OWN), OWN)
    their_rows = pl.ds(pl.multiple_of(other * OWN, OWN), OWN)
    tok_here = copy_here(tokens.at[own_rows], tok.at[c])
    curv_here = copy_here(curvature.at[own_rows], curv.at[c])
    up_here = [copy_here(up_weight, w_up.at[c]), copy_here(up_tangent, w_ut.at[c])]
    down_here = [copy_here(down_weight, w_dn.at[c]), copy_here(down_tangent, w_dt.at[c])]
    barrier = pltpu.get_barrier_semaphore()
    peers = [sibling] + [at_x(k) for k in range(1, NX)] + [at_z(k) for k in range(1, NZ)] + [at_y(k) for k in range(1, NY)]
    for peer in peers:
        pl.semaphore_signal(barrier, inc=1, device_id=peer, device_id_type=MESH)
    pl.semaphore_wait(barrier, len(peers))

    tok_slot, params_slot, curv_slot = fresh("recv"), fresh("recv", 3), fresh("recv")
    up_slot, down_slot = fresh("recv"), fresh("recv")
    copy_to(tokens.at[their_rows], tok.at[c], sibling, sends_of(tok.at[c]), tok_slot)
    for i, (mine, theirs) in enumerate(((gain_in, gin_x), (shift_in, sin_x), (gain_out, gout_x))):
        copy_to(mine, theirs, sibling, sends_of(theirs), params_slot + i)

    def send_weights(pairs, whole, slot):
        sent = sends_of(whole)
        for mine, theirs in pairs:
            copy_to(mine, theirs.at[c], sibling, sent, slot)

    tok_here.wait()
    arrived(tok.at[other], tok_slot)
    source = tok[...].astype(f32)
    total = row_sum(source)
    spread = source - (total / (2 * W))[None]
    stat_a[0] = columns([total, row_sum(spread * spread)])
    stat_slot, sent = fresh("recv"), sends_of(stat_a.at[pl.ds(1, 3)])
    for k in J_ORDER:
        copy_to(stat_a.at[0], stat_a.at[k], at_y(k), sent, stat_slot)
    arrived(gin_x, params_slot)
    arrived(sin_x, params_slot + 1)
    arrived(gout_x, params_slot + 2)

    def by_half(mine, theirs):
        mine, theirs = mine[...].reshape(1, W), theirs[...].reshape(1, W)
        first = jnp.where(c == 0, mine, theirs)
        second = jnp.where(c == 0, theirs, mine)
        return jnp.stack([first, second])

    gain, shift = by_half(gain_in, gin_x), by_half(shift_in, sin_x)
    arrived(stat_a.at[pl.ds(1, 3)], stat_slot)
    totals = [stat_a[k][:, 0:1] for k in range(NY)]
    center = (totals[0] + totals[1] + totals[2] + totals[3]) / D
    variance = jnp.zeros_like(center)
    for k in range(NY):
        off = totals[k] / (2 * W) - center
        variance = variance + stat_a[k][:, 1:2] + (2 * W) * (off * off)
    inverse = lax.rsqrt(variance / D + epsilon)
    def group(k):
        return pl.ds(pl.multiple_of(lax.rem(z + NZ + k, NZ) * GROUP, GROUP), GROUP)

    def block_of(j, k):
        first = lax.rem(z + NZ + k, NZ) * GROUP + lax.rem(x + NX + j, NX) * OWN
        return pl.ds(pl.multiple_of(first, OWN), OWN)

    block = block_of(0, 0)
    normed[:, block] = ((source - center[None]) * inverse[None] * gain + shift).astype(bf16)

    def three_of(offset):
        first = lax.rem(z + NZ + offset, NZ) * GROUP
        return pl.ds(pl.multiple_of(first, GROUP), GROUP - OWN)

    def gather_start(array, far, between):
        sent = sends_of(array.at[:, pl.ds(0, ROWS - OWN)])

        def send(rows, device, slot):
            copy_to(array.at[:, rows], array.at[:, rows], device, sent, slot)

        z_slot, x_slot, last_slot = fresh("recv", NZ), fresh("recv", NX), fresh("recv", NZ)
        for j in J_ORDER:
            send(block, at_x(j), x_slot + j)
        for k in NEAR + far:
            send(block, at_z(k), last_slot + k if k in NEAR else z_slot + k)
        between()
        for j in (1, 3, 2):
            rows = block_of(-j, 0)
            arrived(array.at[:, rows], x_slot + j)
            for k in NEAR:
                send(rows, at_z(k), last_slot + k)
        for k in far:
            rows = block_of(0, -k)
            arrived(array.at[:, rows], z_slot + k)
            for j in J_ORDER:
                send(rows, at_x(j), last_slot + k)
        return last_slot

    def gather_wait(array, last_slot, chunk):
        for offset in chunk:
            k = (NZ - offset) % NZ
            if k in NEAR:
                arrived(array.at[:, group(-k)], last_slot + k)
            elif k:
                arrived(array.at[:, three_of(-k)], last_slot + k)

    def stacked(array, chunk):
        parts = [array[group(offset)] for offset in chunk]
        return parts[0] if len(parts) == 1 else jnp.concatenate(parts, axis=0)

    normed_slots = gather_start(
        normed, (4, 3, 5, 2, 6), lambda: send_weights(((up_weight, w_up), (up_tangent, w_ut)), w_up, up_slot)
    )
    send_weights(((down_weight, w_dn), (down_tangent, w_dt)), w_dn, down_slot)
    copy_to(curvature.at[their_rows], curv.at[c], sibling, sends_of(curv.at[c]), curv_slot)

    share_slot, share_sent = fresh("recv", NZ), sends_of(part_s)
    both_slot, both_sent = fresh("recv", NZ), sends_of(both.at[:, pl.ds(0, ROWS - NZ * OWN)])
    normed_x_slot, hidden_x_slot = fresh("recv"), fresh("recv")
    raw_slot, raw_sent = fresh("recv", 2), sends_of(raw_s)
    out_slot, out_sent = fresh("recv", 6), sends_of(out_s)
    sum_slot, sum_sent = fresh("recv"), sends_of(sum_s)
    ordered = (0,) + FAR

    def up_step(name):
        chunk = FORWARD[name]
        size = len(chunk)
        gather_wait(normed, normed_slots, chunk)
        if up_here:
            while up_here:
                up_here.pop().wait()
            arrived(w_up, up_slot)
        left, right = stacked(normed.at[0], chunk), stacked(normed.at[1], chunk)
        rows = pl.ds(0, size * GROUP)
        part_f[0, rows] = dot(left, w_up[0]) + dot(right, w_up[1])
        part_f[1, rows] = dot(left, w_ut[0]) + dot(right, w_ut[1])

        def share(i, j):
            mine = lax.rem(y + j, NY) * OWN
            return part_f[:, pl.ds(pl.multiple_of(i * GROUP + mine, OWN), OWN)]

        for j in J_ORDER:
            for i, offset in enumerate(chunk):
                part_s[offset, j - 1] = share(i, j).astype(bf16)
                copy_to(part_s.at[offset, j - 1], part_r.at[offset, j - 1], at_y(j), share_sent, share_slot + offset)
        for i, offset in enumerate(chunk):
            part_own[offset] = share(i, 0)

    def share_rows(offset, who):
        first = lax.rem(z + offset, NZ) * GROUP + lax.rem(who + NY, NY) * OWN
        return pl.ds(pl.multiple_of(first, OWN), OWN)

    def act_step(name):
        for offset in FORWARD[name]:
            arrived(part_r.at[offset], share_slot + offset)
            sums = part_own[offset]
            for j in range(1, NY):
                sums = sums + part_r[offset, j - 1].astype(f32)
            pre = sums[0] + up_bias[...].reshape(1, W)
            phi = 0.5 * (1.0 + lax.erf(pre * root_half))
            derivative = phi + pre * jnp.exp(-0.5 * pre * pre) * inv_root_two_pi
            rows = share_rows(offset, y)
            both[0, rows] = (pre * phi).astype(bf16)
            both[1, rows] = (derivative * sums[1]).astype(bf16)
            slope[offset] = derivative.astype(bf16)
            for j in J_ORDER:
                copy_to(both.at[:, rows], both.at[:, rows], at_y(j), both_sent, both_slot + offset)

    def down_step(name):
        chunk = FORWARD[name]
        for offset in chunk:
            arrived(both.at[:, three_of(offset)], both_slot + offset)
        if down_here:
            while down_here:
                down_here.pop().wait()
            arrived(w_dn, down_slot)
        hidden, hidden_tangent = stacked(both.at[0], chunk), stacked(both.at[1], chunk)
        rows = pl.ds(0, len(chunk) * GROUP)
        for f in range(2):
            out_f[0, f, rows] = dot(hidden, w_dn[f])
            out_f[1, f, rows] = dot(hidden_tangent, w_dn[f]) + dot(hidden, w_dt[f])
        for i, offset in enumerate(chunk):
            if offset in NEAR:
                at = NEAR.index(offset)
                raw_s[at] = out_f[:, :, pl.ds(i * GROUP, GROUP)].astype(bf16)
                copy_to(raw_s.at[at], raw_r.at[at], at_z(offset), raw_sent, raw_slot + at)
                continue
            at = ordered.index(offset)
            if offset == 0:
                for k in range(len(NEAR)):
                    arrived(raw_r.at[k], raw_slot + k)

            def part(j):
                first = pl.multiple_of(lax.rem(x + j, NX) * OWN, OWN)
                value = out_f[:, :, pl.ds(first, OWN)]
                if offset == 0:
                    for k in range(len(NEAR)):
                        value = value + raw_r[k, :, :, pl.ds(first, OWN)].astype(f32)
                return value

            for j in J_ORDER:
                out_s[at, j - 1] = part(j).astype(bf16)
                copy_to(out_s.at[at, j - 1], out_r.at[at, j - 1], at_x(j), out_sent, out_slot + at)
            own_x[at] = part(0)

    def summed(offset):
        at = ordered.index(offset)
        arrived(out_r.at[at], out_slot + at)
        value = own_x[at]
        for j in range(1, NX):
            value = value + out_r[at, j - 1].astype(f32)
        return value

    def sum_step(name):
        for offset in FORWARD[name]:
            at = FAR.index(offset)
            sum_s[at] = summed(offset).astype(bf16)
            copy_to(sum_s.at[at], sum_r.at[at], at_z(offset), sum_sent, sum_slot)

    steps = {"u": up_step, "a": act_step, "d": down_step, "s": sum_step}
    order = (
        "u0", "u17", "u4", "u3", "a17", "a4", "u5", "a3", "d17", "d4", "u2", "a5", "d3",
        "u6", "a2", "d5", "s4", "a6", "s3", "a0", "d2", "s5", "d6", "s2", "d0", "s6",
    )
    for step in order:
        if step == "d2":
            copy_to(normed.at[other], normed_x_out, sibling, sends_of(normed.at[other]), normed_x_slot)
            normed_written = copy_here(normed.at[c], normed_out)
            for f in range(2):
                w_dn_t[f] = w_dn[f].T
        steps[step[0]](step[1:])
    copy_to(both.at[0], hidden_x, sibling, sends_of(both.at[0]), hidden_x_slot)

    arrived(curv.at[other], curv_slot)
    curv_here.wait()
    gain = by_half(gain_out, gout_x)
    factor = gain * gain * curv[...]
    outputs = summed(0)
    arrived(sum_r, sum_slot)
    for k in range(len(FAR)):
        outputs = outputs + sum_r[k].astype(f32)

    output = tok[...].astype(f32) + outputs[0]
    tangent = outputs[1]
    total = row_sum(output)
    around = output - (total / (2 * W))[None]
    factor_around = factor * around
    stat_b[0] = columns([
        total, row_sum(around * around), row_sum(tangent), row_sum(around * tangent),
        row_sum(factor), row_sum(factor_around), row_sum(factor_around * around),
        row_sum(factor * tangent), row_sum(factor_around * tangent),
    ])
    stat_slot, sent = fresh("recv"), sends_of(stat_b.at[pl.ds(1, 3)])
    for k in J_ORDER:
        copy_to(stat_b.at[0], stat_b.at[k], at_y(k), sent, stat_slot)
    arrived(stat_b.at[pl.ds(1, 3)], stat_slot)
    stats = [[stat_b[k][:, i:i + 1] for i in range(9)] for k in range(NY)]
    center = (stats[0][0] + stats[1][0] + stats[2][0] + stats[3][0]) / D
    zero = jnp.zeros_like(center)
    square, sum_t, dot_t, f_0, f_1, f_2, ft_0, ft_1 = (zero,) * 8
    for s in stats:
        off = s[0] / (2 * W) - center
        square = square + s[1] + (2 * W) * (off * off)
        sum_t = sum_t + s[2]
        dot_t = dot_t + s[3] + off * s[2]
        f_0 = f_0 + s[4]
        f_1 = f_1 + s[5] + off * s[4]
        f_2 = f_2 + s[6] + 2.0 * off * s[5] + off * off * s[4]
        ft_0 = ft_0 + s[7]
        ft_1 = ft_1 + s[8] + off * s[7]
    inverse = lax.rsqrt(square / D + epsilon)
    mean_t = sum_t / D
    mean_nt = dot_t * inverse / D
    fn_1 = f_1 * inverse
    mean_w = (ft_0 - mean_t * f_0 - mean_nt * fn_1) * inverse / D
    mean_nw = (ft_1 * inverse - mean_t * fn_1 - mean_nt * (f_2 * inverse * inverse)) * inverse / D
    normal = (output - center[None]) * inverse[None]
    weighted = factor * ((tangent - mean_t[None] - normal * mean_nt[None]) * inverse[None])
    cot[:, block] = ((weighted - mean_w[None] - normal * mean_nw[None]) * inverse[None]).astype(bf16)

    cot_slots = gather_start(cot, FAR[::-1], lambda: None)
    back_slot, back_sent = fresh("recv", NZ), sends_of(back_s)
    grad_slot, grad_sent = fresh("recv", NZ), sends_of(grad.at[pl.ds(0, ROWS - NZ * OWN)])
    cot_x_slot, cot_x_sent = fresh("recv"), sends_of(cot.at[other])
    grad_x_slot, grad_x_sent = fresh("recv"), sends_of(grad)
    grad_written = fresh("local")

    def back_step(name):
        chunk = BACKWARD[name]
        size = len(chunk)
        gather_wait(cot, cot_slots, chunk)
        left, right = stacked(cot.at[0], chunk), stacked(cot.at[1], chunk)
        back_f[pl.ds(0, size * GROUP)] = dot(left, w_dn_t[0]) + dot(right, w_dn_t[1])

        def share(i, j):
            mine = lax.rem(y + j, NY) * OWN
            return back_f[pl.ds(pl.multiple_of(i * GROUP + mine, OWN), OWN)]

        for j in J_ORDER:
            for i, offset in enumerate(chunk):
                back_s[offset, j - 1] = share(i, j).astype(bf16)
                copy_to(back_s.at[offset, j - 1], back_r.at[offset, j - 1], at_y(j), back_sent, back_slot + offset)
        for i, offset in enumerate(chunk):
            back_own[offset] = share(i, 0)
            rows = group(offset)
            copy_to(cot.at[other, rows], cot_x.at[rows], sibling, cot_x_sent, cot_x_slot)

    def grad_step(name):
        for offset in BACKWARD[name]:
            arrived(back_r.at[offset], back_slot + offset)
            sums = back_own[offset]
            for j in range(1, NY):
                sums = sums + back_r[offset, j - 1].astype(f32)
            rows = share_rows(offset, y)
            grad[rows] = (sums * slope[offset].astype(f32)).astype(bf16)
            for j in J_ORDER:
                copy_to(grad.at[rows], grad.at[rows], at_y(j), grad_sent, grad_slot + offset)

    def swap_step(name):
        for offset in BACKWARD[name]:
            arrived(grad.at[three_of(offset)], grad_slot + offset)
            rows = group(offset)
            copy_to(grad.at[rows], grad_x_out.at[rows], sibling, grad_x_sent, grad_x_slot)
            copy = pltpu.make_async_copy(grad.at[rows], grad_out.at[rows], local_sem.at[grad_written])
            copy.start()

    steps = {"b": back_step, "g": grad_step, "w": swap_step}
    for step in ("b0", "b17", "g0", "b26", "g17", "b35", "b4", "g26", "g35", "g4", "w0", "w17", "w26"):
        steps[step[0]](step[1:])
    arrived(hidden_x, hidden_x_slot)
    arrived(cot_x, cot_x_slot)
    written = [normed_written]
    for n in range(TILES):
        part = pl.ds(n * TILE, TILE)
        stage[part] = dot_first(both[0, :, part], cot[c]) + dot_first(hidden_x[:, part], cot_x[...])
        written.append(copy_here(stage.at[part], down_out.at[part]))
    swap_step("35")
    swap_step("4")
    arrived(normed_x_out, normed_x_slot)
    for copy in written:
        copy.wait()
    for ref, slot in ends:
        bytes_of(ref, slot, 0).wait_send()
    pltpu.make_async_copy(grad, grad_out, local_sem.at[grad_written]).wait()
    arrived(grad_x_out, grad_x_slot)
    assert counts["send"] <= N_SEND and counts["recv"] <= N_RECV and counts["local"] <= N_LOCAL


def finish_kernel(down, normed, normed_x, grad, grad_x, up_out, down_out, n_own, n_x, g_own, g_x, moving, stage, sems):
    pairs = ((normed, n_own), (grad, g_own), (normed_x, n_x), (grad_x, g_x), (down, moving))
    loads = [pltpu.make_async_copy(src, dst, sems.at[i]) for i, (src, dst) in enumerate(pairs)]
    for copy in loads:
        copy.start()
    for copy in loads[:2]:
        copy.wait()
    for n in range(TILES):
        part = pl.ds(n * TILE, TILE)
        stage[part] = dot_first(n_own[:, part], g_own[...])
    for copy in loads[2:]:
        copy.wait()
    moved = pltpu.make_async_copy(moving, down_out, sems.at[0])
    moved.start()
    written = [moved]
    for n in range(TILES):
        part = pl.ds(n * TILE, TILE)
        stage[part] += dot_first(n_x[:, part], g_x[...])
        copy = pltpu.make_async_copy(stage.at[part], up_out.at[part], sems.at[5 + n])
        copy.start()
        written.append(copy)
    for copy in written:
        copy.wait()


def on_device(*args):
    any_ = pl.BlockSpec(memory_space=pl.ANY)
    vmem = pl.BlockSpec(memory_space=pltpu.VMEM)
    scratch = [
        ((2, W, W), bf16), ((2, W, W), bf16), ((2, W, W), bf16), ((2, W, W), bf16),
        ((2, OWN, W), bf16), ((2, OWN, W), f32), ((W,), f32), ((W,), f32), ((W,), f32),
        ((NY, OWN, 128), f32), ((NY, OWN, 128), f32),
        ((2, ROWS, W), bf16),
        ((2, 2 * GROUP, W), f32), ((NZ, 3, 2, OWN, W), bf16), ((NZ, 3, 2, OWN, W), bf16), ((NZ, 2, OWN, W), f32),
        ((2, ROWS, W), bf16), ((ROWS, W), bf16), ((NZ, OWN, W), bf16),
        ((2, 2, 2 * GROUP, W), f32), ((2, 2, 2, GROUP, W), bf16), ((2, 2, 2, GROUP, W), bf16),
        ((6, 2, 2, OWN, W), f32), ((6, 3, 2, 2, OWN, W), bf16), ((6, 3, 2, 2, OWN, W), bf16),
        ((5, 2, 2, OWN, W), bf16), ((5, 2, 2, OWN, W), bf16),
        ((2, ROWS, W), bf16), ((ROWS, W), bf16),
        ((2 * GROUP, W), f32), ((NZ, 3, OWN, W), bf16), ((NZ, 3, OWN, W), bf16), ((NZ, OWN, W), f32),
        ((ROWS, W), bf16), ((W, W), f32), ((2, W, W), bf16),
    ]
    product = jax.ShapeDtypeStruct((W, W), f32)
    rows = jax.ShapeDtypeStruct((ROWS, W), bf16)
    partial = pl.pallas_call(
        kernel,
        out_shape=(product, rows, rows, rows, rows),
        in_specs=[any_, vmem, vmem, any_, vmem, any_, vmem, any_, any_, any_],
        out_specs=(any_,) * 5,
        scratch_shapes=[pltpu.VMEM(shape, dtype) for shape, dtype in scratch]
        + [pltpu.SemaphoreType.DMA((N_SEND,)), pltpu.SemaphoreType.DMA((N_RECV,)), pltpu.SemaphoreType.DMA((N_LOCAL,))],
        compiler_params=pltpu.CompilerParams(
            collective_id=0, has_side_effects=True, vmem_limit_bytes=60 * 2**20
        ),
        cost_estimate=pl.CostEstimate(flops=9663676416, bytes_accessed=9437184, transcendentals=262144),
        name="gauss_newton",
    )(*args)
    return pl.pallas_call(
        finish_kernel,
        out_shape=(product, product),
        in_specs=[any_] * 5,
        out_specs=(any_, any_),
        scratch_shapes=[pltpu.VMEM((ROWS, W), bf16)] * 4
        + [pltpu.VMEM((W, W), f32)] * 2
        + [pltpu.SemaphoreType.DMA((8,))],
        compiler_params=pltpu.CompilerParams(vmem_limit_bytes=60 * 2**20),
        cost_estimate=pl.CostEstimate(flops=1207959552, bytes_accessed=10223616, transcendentals=0),
        name="finish",
    )(*partial)


def solution(mesh):
    return jax.shard_map(
        on_device,
        mesh=mesh,
        in_specs=(
            P("dp", "tensor"),
            P("tensor"),
            P("tensor"),
            P("tensor", "dp"),
            P("dp"),
            P("dp", "tensor"),
            P("tensor"),
            P("dp", "tensor"),
            P("tensor", "dp"),
            P("dp", "tensor"),
        ),
        out_specs=(P("tensor", "dp"), P("dp", "tensor")),
        check_vma=False,
    )
```

```python
import functools

import jax
import jax.numpy as jnp
from jax import lax
from jax.experimental import pallas as pl
from jax.experimental.pallas import tpu as pltpu
from jax.sharding import PartitionSpec as P

D = 6144
epsilon = 1e-05
root_half = 0.7071067811865476
inv_root_two_pi = 0.3989422804014327

f32 = jnp.float32
bf16 = jnp.bfloat16
MESH = pl.DeviceIdType.MESH

NX, NZ, NY = 4, 8, 4
OWN = 16
GROUP = NX * OWN
ROWS = NZ * GROUP
W = 768
TILE = 256
TILES = W // TILE
FORWARD = {"0": (0,), "4": (4,), "17": (1, 7), "3": (3,), "5": (5,), "2": (2,), "6": (6,)}
BACKWARD = {"0": (0,), "17": (1, 7), "6": (6,), "2": (2,), "5": (5,), "3": (3,), "4": (4,)}
NEAR = (1, 7)
FAR = (4, 3, 5, 2, 6)
J_ORDER = (2, 1, 3)

N_SEND = 22
N_RECV = 94
N_LOCAL = 11


def dot(a, b):
    return jnp.dot(a, b, preferred_element_type=f32)


def dot_last(a, b):
    return lax.dot_general(a, b, (((1,), (1,)), ((), ())), preferred_element_type=f32)


def dot_first(a, b):
    return lax.dot_general(a, b, (((0,), (0,)), ((), ())), preferred_element_type=f32)


def columns(values):
    lane = lax.broadcasted_iota(jnp.int32, (OWN, 128), 1)
    out = jnp.zeros((OWN, 128), f32)
    for at, value in enumerate(values):
        out = jnp.where(lane == at, value, out)
    return out


def row_sum(pair):
    return jnp.sum(pair[0] + pair[1], axis=1, keepdims=True)


def kernel(
    tokens, gain_in, shift_in, up_weight, up_bias, down_weight, gain_out, curvature, up_tangent, down_tangent,
    down_out, normed_out, normed_x_out, grad_out, grad_x_out,
    w_up, w_ut, w_dn, w_dt, tok, curv, gin_x, sin_x, gout_x,
    stat_a, stat_b, normed, part_f, part_s, part_r, part_own,
    both, hidden_x, slope, out_f, raw_s, raw_r, own_x, out_s, out_r, sum_s, sum_r,
    cot, cot_x, back_f, back_s, back_r, back_own, grad, stage, w_dn_t,
    send_sem, recv_sem, local_sem,
):
    d, t = lax.axis_index("dp"), lax.axis_index("tensor")
    x, z = d // NZ, lax.rem(d, NZ)
    y, c = t // 2, lax.rem(t, 2)
    other = 1 - c

    def at_x(k):
        return (lax.rem(x + k, NX) * NZ + z, t)

    def at_z(k):
        return (x * NZ + lax.rem(z + k, NZ), t)

    def at_y(k):
        return (d, lax.rem(y + k, NY) * 2 + c)

    sibling = (d, y * 2 + other)
    ends, counts = [], {"send": 0, "recv": 0, "local": 0}

    def fresh(kind, n=1):
        at = counts[kind]
        counts[kind] += n
        return at

    def sends_of(ref):
        slot = fresh("send")
        ends.append((ref, slot))
        return slot

    def copy_to(src, dst, device, sent, slot):
        pltpu.make_async_remote_copy(
            src_ref=src, dst_ref=dst, send_sem=send_sem.at[sent],
            recv_sem=recv_sem.at[slot], device_id=device, device_id_type=MESH,
        ).start()

    def bytes_of(ref, sent, slot):
        return pltpu.make_async_remote_copy(
            src_ref=ref, dst_ref=ref, send_sem=send_sem.at[sent],
            recv_sem=recv_sem.at[slot], device_id=sibling, device_id_type=MESH,
        )

    def arrived(ref, slot):
        bytes_of(ref, 0, slot).wait_recv()

    def copy_here(src, dst):
        copy = pltpu.make_async_copy(src, dst, local_sem.at[fresh("local")])
        copy.start()
        return copy

    own_rows = pl.ds(pl.multiple_of(c * OWN, OWN), OWN)
    their_rows = pl.ds(pl.multiple_of(other * OWN, OWN), OWN)
    tok_here = copy_here(tokens.at[own_rows], tok.at[c])
    curv_here = copy_here(curvature.at[own_rows], curv.at[c])
    up_here = [copy_here(up_weight, w_up.at[c]), copy_here(up_tangent, w_ut.at[c])]
    down_here = [copy_here(down_weight, w_dn.at[c]), copy_here(down_tangent, w_dt.at[c])]
    barrier = pltpu.get_barrier_semaphore()
    peers = [sibling] + [at_x(k) for k in range(1, NX)] + [at_z(k) for k in range(1, NZ)] + [at_y(k) for k in range(1, NY)]
    for peer in peers:
        pl.semaphore_signal(barrier, inc=1, device_id=peer, device_id_type=MESH)
    pl.semaphore_wait(barrier, len(peers))

    tok_slot, params_slot, curv_slot = fresh("recv"), fresh("recv", 3), fresh("recv")
    up_slot, down_slot = fresh("recv"), fresh("recv")
    copy_to(tokens.at[their_rows], tok.at[c], sibling, sends_of(tok.at[c]), tok_slot)
    for i, (mine, theirs) in enumerate(((gain_in, gin_x), (shift_in, sin_x), (gain_out, gout_x))):
        copy_to(mine, theirs, sibling, sends_of(theirs), params_slot + i)

    def send_weights(pairs, whole, slot):
        sent = sends_of(whole)
        for mine, theirs in pairs:
            copy_to(mine, theirs.at[c], sibling, sent, slot)

    tok_here.wait()
    arrived(tok.at[other], tok_slot)
    source = tok[...].astype(f32)
    total = row_sum(source)
    spread = source - (total / (2 * W))[None]
    stat_a[0] = columns([total, row_sum(spread * spread)])
    stat_slot, sent = fresh("recv"), sends_of(stat_a.at[pl.ds(1, 3)])
    for k in J_ORDER:
        copy_to(stat_a.at[0], stat_a.at[k], at_y(k), sent, stat_slot)
    arrived(gin_x, params_slot)
    arrived(sin_x, params_slot + 1)
    arrived(gout_x, params_slot + 2)

    def by_half(mine, theirs):
        mine, theirs = mine[...].reshape(1, W), theirs[...].reshape(1, W)
        first = jnp.where(c == 0, mine, theirs)
        second = jnp.where(c == 0, theirs, mine)
        return jnp.stack([first, second])

    gain, shift = by_half(gain_in, gin_x), by_half(shift_in, sin_x)
    arrived(stat_a.at[pl.ds(1, 3)], stat_slot)
    totals = [stat_a[k][:, 0:1] for k in range(NY)]
    center = (totals[0] + totals[1] + totals[2] + totals[3]) / D
    variance = jnp.zeros_like(center)
    for k in range(NY):
        off = totals[k] / (2 * W) - center
        variance = variance + stat_a[k][:, 1:2] + (2 * W) * (off * off)
    inverse = lax.rsqrt(variance / D + epsilon)
    def group(k):
        return pl.ds(pl.multiple_of(lax.rem(z + NZ + k, NZ) * GROUP, GROUP), GROUP)

    def block_of(j, k):
        first = lax.rem(z + NZ + k, NZ) * GROUP + lax.rem(x + NX + j, NX) * OWN
        return pl.ds(pl.multiple_of(first, OWN), OWN)

    block = block_of(0, 0)
    normed[:, block] = ((source - center[None]) * inverse[None] * gain + shift).astype(bf16)

    def three_of(offset):
        first = lax.rem(z + NZ + offset, NZ) * GROUP
        return pl.ds(pl.multiple_of(first, GROUP), GROUP - OWN)

    def gather_start(array, far, between, relay):
        sent = sends_of(array.at[:, pl.ds(0, ROWS - OWN)])

        def send(rows, device, slot):
            copy_to(array.at[:, rows], array.at[:, rows], device, sent, slot)

        z_slot, x_slot, last_slot = fresh("recv", NZ), fresh("recv", NX), fresh("recv", NZ)
        for j in J_ORDER:
            send(block, at_x(j), x_slot + j)
        for k in (4,) + NEAR if relay else NEAR + far:
            send(block, at_z(k), z_slot + k)
        between()
        for k, onward in ((1, ((1, 2), (2, 3))), (7, ((7, 6), (6, 5)))):
            rows = block_of(0, -k)
            arrived(array.at[:, rows], z_slot + k)
            for step, total in onward if relay else ():
                send(rows, at_z(step), z_slot + total)
        for j in (1, 3, 2):
            rows = block_of(-j, 0)
            arrived(array.at[:, rows], x_slot + j)
            for k in NEAR:
                send(rows, at_z(k), last_slot + k)
        for k in far:
            rows = block_of(0, -k)
            arrived(array.at[:, rows], z_slot + k)
            for j in J_ORDER:
                send(rows, at_x(j), last_slot + k)
        return last_slot

    def gather_wait(array, last_slot, chunk):
        for offset in chunk:
            k = (NZ - offset) % NZ
            if k in NEAR:
                arrived(array.at[:, three_of(-k)], last_slot + k)
            elif k:
                arrived(array.at[:, three_of(-k)], last_slot + k)

    def stacked(array, chunk):
        parts = [array[group(offset)] for offset in chunk]
        return parts[0] if len(parts) == 1 else jnp.concatenate(parts, axis=0)

    normed_slots = gather_start(
        normed, (4, 3, 5, 2, 6), lambda: send_weights(((up_weight, w_up), (up_tangent, w_ut)), w_up, up_slot), True
    )
    send_weights(((down_weight, w_dn), (down_tangent, w_dt)), w_dn, down_slot)
    copy_to(curvature.at[their_rows], curv.at[c], sibling, sends_of(curv.at[c]), curv_slot)

    share_slot, share_sent = fresh("recv", NZ), sends_of(part_s)
    both_slot, both_sent = fresh("recv", NZ), sends_of(both.at[:, pl.ds(0, ROWS - NZ * OWN)])
    normed_x_slot, hidden_x_slot = fresh("recv"), fresh("recv")
    raw_slot, raw_sent = fresh("recv", 2), sends_of(raw_s)
    out_slot, out_sent = fresh("recv", 6), sends_of(out_s)
    sum_slot, sum_sent = fresh("recv"), sends_of(sum_s)
    ordered = (0,) + FAR

    def up_step(name):
        chunk = FORWARD[name]
        size = len(chunk)
        gather_wait(normed, normed_slots, chunk)
        if up_here:
            while up_here:
                up_here.pop().wait()
            arrived(w_up, up_slot)
        left, right = stacked(normed.at[0], chunk), stacked(normed.at[1], chunk)
        rows = pl.ds(0, size * GROUP)
        part_f[0, rows] = dot(left, w_up[0]) + dot(right, w_up[1])
        part_f[1, rows] = dot(left, w_ut[0]) + dot(right, w_ut[1])

        def share(i, j):
            mine = lax.rem(y + j, NY) * OWN
            return part_f[:, pl.ds(pl.multiple_of(i * GROUP + mine, OWN), OWN)]

        for j in J_ORDER:
            for i, offset in enumerate(chunk):
                part_s[offset, j - 1] = share(i, j).astype(bf16)
                copy_to(part_s.at[offset, j - 1], part_r.at[offset, j - 1], at_y(j), share_sent, share_slot + offset)
        for i, offset in enumerate(chunk):
            part_own[offset] = share(i, 0)

    def share_rows(offset, who):
        first = lax.rem(z + offset, NZ) * GROUP + lax.rem(who + NY, NY) * OWN
        return pl.ds(pl.multiple_of(first, OWN), OWN)

    def act_step(name):
        for offset in FORWARD[name]:
            arrived(part_r.at[offset], share_slot + offset)
            sums = part_own[offset]
            for j in range(1, NY):
                sums = sums + part_r[offset, j - 1].astype(f32)
            pre = sums[0] + up_bias[...].reshape(1, W)
            phi = 0.5 * (1.0 + lax.erf(pre * root_half))
            derivative = phi + pre * jnp.exp(-0.5 * pre * pre) * inv_root_two_pi
            rows = share_rows(offset, y)
            both[0, rows] = (pre * phi).astype(bf16)
            both[1, rows] = (derivative * sums[1]).astype(bf16)
            slope[offset] = derivative.astype(bf16)
            for j in J_ORDER:
                copy_to(both.at[:, rows], both.at[:, rows], at_y(j), both_sent, both_slot + offset)

    def down_step(name):
        chunk = FORWARD[name]
        for offset in chunk:
            arrived(both.at[:, three_of(offset)], both_slot + offset)
        if down_here:
            while down_here:
                down_here.pop().wait()
            arrived(w_dn, down_slot)
        hidden, hidden_tangent = stacked(both.at[0], chunk), stacked(both.at[1], chunk)
        rows = pl.ds(0, len(chunk) * GROUP)
        for f in range(2):
            out_f[0, f, rows] = dot(hidden, w_dn[f])
            out_f[1, f, rows] = dot(hidden_tangent, w_dn[f]) + dot(hidden, w_dt[f])
        for i, offset in enumerate(chunk):
            if offset in NEAR:
                at = NEAR.index(offset)
                raw_s[at] = out_f[:, :, pl.ds(i * GROUP, GROUP)].astype(bf16)
                copy_to(raw_s.at[at], raw_r.at[at], at_z(offset), raw_sent, raw_slot + at)
                continue
            at = ordered.index(offset)
            if offset == 0:
                for k in range(len(NEAR)):
                    arrived(raw_r.at[k], raw_slot + k)

            def part(j):
                first = pl.multiple_of(lax.rem(x + j, NX) * OWN, OWN)
                value = out_f[:, :, pl.ds(first, OWN)]
                if offset == 0:
                    for k in range(len(NEAR)):
                        value = value + raw_r[k, :, :, pl.ds(first, OWN)].astype(f32)
                return value

            for j in J_ORDER:
                out_s[at, j - 1] = part(j).astype(bf16)
                copy_to(out_s.at[at, j - 1], out_r.at[at, j - 1], at_x(j), out_sent, out_slot + at)
            own_x[at] = part(0)

    def summed(offset):
        at = ordered.index(offset)
        arrived(out_r.at[at], out_slot + at)
        value = own_x[at]
        for j in range(1, NX):
            value = value + out_r[at, j - 1].astype(f32)
        return value

    def sum_step(name):
        for offset in FORWARD[name]:
            at = FAR.index(offset)
            sum_s[at] = summed(offset).astype(bf16)
            copy_to(sum_s.at[at], sum_r.at[at], at_z(offset), sum_sent, sum_slot)

    steps = {"u": up_step, "a": act_step, "d": down_step, "s": sum_step}
    order = (
        "u0", "u17", "u4", "u3", "a17", "a4", "u5", "a3", "d17", "d4", "u2", "a5", "d3",
        "u6", "a2", "d5", "s4", "a6", "s3", "a0", "d2", "s5", "d6", "s2", "d0", "s6",
    )
    for step in order:
        if step == "d2":
            copy_to(normed.at[other], normed_x_out, sibling, sends_of(normed.at[other]), normed_x_slot)
            normed_written = copy_here(normed.at[c], normed_out)
            for f in range(2):
                w_dn_t[f] = w_dn[f].T
        steps[step[0]](step[1:])
    copy_to(both.at[0], hidden_x, sibling, sends_of(both.at[0]), hidden_x_slot)

    arrived(curv.at[other], curv_slot)
    curv_here.wait()
    gain = by_half(gain_out, gout_x)
    factor = gain * gain * curv[...]
    outputs = summed(0)
    arrived(sum_r, sum_slot)
    for k in range(len(FAR)):
        outputs = outputs + sum_r[k].astype(f32)

    output = tok[...].astype(f32) + outputs[0]
    tangent = outputs[1]
    total = row_sum(output)
    around = output - (total / (2 * W))[None]
    factor_around = factor * around
    stat_b[0] = columns([
        total, row_sum(around * around), row_sum(tangent), row_sum(around * tangent),
        row_sum(factor), row_sum(factor_around), row_sum(factor_around * around),
        row_sum(factor * tangent), row_sum(factor_around * tangent),
    ])
    stat_slot, sent = fresh("recv"), sends_of(stat_b.at[pl.ds(1, 3)])
    for k in J_ORDER:
        copy_to(stat_b.at[0], stat_b.at[k], at_y(k), sent, stat_slot)
    arrived(stat_b.at[pl.ds(1, 3)], stat_slot)
    stats = [[stat_b[k][:, i:i + 1] for i in range(9)] for k in range(NY)]
    center = (stats[0][0] + stats[1][0] + stats[2][0] + stats[3][0]) / D
    zero = jnp.zeros_like(center)
    square, sum_t, dot_t, f_0, f_1, f_2, ft_0, ft_1 = (zero,) * 8
    for s in stats:
        off = s[0] / (2 * W) - center
        square = square + s[1] + (2 * W) * (off * off)
        sum_t = sum_t + s[2]
        dot_t = dot_t + s[3] + off * s[2]
        f_0 = f_0 + s[4]
        f_1 = f_1 + s[5] + off * s[4]
        f_2 = f_2 + s[6] + 2.0 * off * s[5] + off * off * s[4]
        ft_0 = ft_0 + s[7]
        ft_1 = ft_1 + s[8] + off * s[7]
    inverse = lax.rsqrt(square / D + epsilon)
    mean_t = sum_t / D
    mean_nt = dot_t * inverse / D
    fn_1 = f_1 * inverse
    mean_w = (ft_0 - mean_t * f_0 - mean_nt * fn_1) * inverse / D
    mean_nw = (ft_1 * inverse - mean_t * fn_1 - mean_nt * (f_2 * inverse * inverse)) * inverse / D
    normal = (output - center[None]) * inverse[None]
    weighted = factor * ((tangent - mean_t[None] - normal * mean_nt[None]) * inverse[None])
    cot[:, block] = ((weighted - mean_w[None] - normal * mean_nw[None]) * inverse[None]).astype(bf16)

    cot_slots = gather_start(cot, FAR[::-1], lambda: None, False)
    back_slot, back_sent = fresh("recv", NZ), sends_of(back_s)
    grad_slot, grad_sent = fresh("recv", NZ), sends_of(grad.at[pl.ds(0, ROWS - NZ * OWN)])
    cot_x_slot, cot_x_sent = fresh("recv"), sends_of(cot.at[other])
    grad_x_slot, grad_x_sent = fresh("recv"), sends_of(grad)
    grad_written = fresh("local")

    def back_step(name):
        chunk = BACKWARD[name]
        size = len(chunk)
        gather_wait(cot, cot_slots, chunk)
        left, right = stacked(cot.at[0], chunk), stacked(cot.at[1], chunk)
        back_f[pl.ds(0, size * GROUP)] = dot(left, w_dn_t[0]) + dot(right, w_dn_t[1])

        def share(i, j):
            mine = lax.rem(y + j, NY) * OWN
            return back_f[pl.ds(pl.multiple_of(i * GROUP + mine, OWN), OWN)]

        for j in J_ORDER:
            for i, offset in enumerate(chunk):
                back_s[offset, j - 1] = share(i, j).astype(bf16)
                copy_to(back_s.at[offset, j - 1], back_r.at[offset, j - 1], at_y(j), back_sent, back_slot + offset)
        for i, offset in enumerate(chunk):
            back_own[offset] = share(i, 0)
            rows = group(offset)
            copy_to(cot.at[other, rows], cot_x.at[rows], sibling, cot_x_sent, cot_x_slot)

    def grad_step(name):
        for offset in BACKWARD[name]:
            arrived(back_r.at[offset], back_slot + offset)
            sums = back_own[offset]
            for j in range(1, NY):
                sums = sums + back_r[offset, j - 1].astype(f32)
            rows = share_rows(offset, y)
            grad[rows] = (sums * slope[offset].astype(f32)).astype(bf16)
            for j in J_ORDER:
                copy_to(grad.at[rows], grad.at[rows], at_y(j), grad_sent, grad_slot + offset)

    def swap_step(name):
        for offset in BACKWARD[name]:
            arrived(grad.at[three_of(offset)], grad_slot + offset)
            rows = group(offset)
            copy_to(grad.at[rows], grad_x_out.at[rows], sibling, grad_x_sent, grad_x_slot)
            copy = pltpu.make_async_copy(grad.at[rows], grad_out.at[rows], local_sem.at[grad_written])
            copy.start()

    written = [normed_written]

    def product_step(_):
        arrived(hidden_x, hidden_x_slot)
        arrived(cot_x, cot_x_slot)
        for n in range(TILES):
            part = pl.ds(n * TILE, TILE)
            stage[part] = dot_first(both[0, :, part], cot[c]) + dot_first(hidden_x[:, part], cot_x[...])
            written.append(copy_here(stage.at[part], down_out.at[part]))

    steps = {"b": back_step, "g": grad_step, "w": swap_step, "p": product_step}
    order = (
        "b0", "b17", "b6", "g0", "b2", "g17", "b5", "g6", "b3", "g2", "b4", "g5",
        "g3", "g4", "w0", "w17", "w6", "p", "w2", "w5", "w3", "w4",
    )
    for step in order:
        steps[step[0]](step[1:])
    arrived(normed_x_out, normed_x_slot)
    for copy in written:
        copy.wait()
    for ref, slot in ends:
        bytes_of(ref, slot, 0).wait_send()
    pltpu.make_async_copy(grad, grad_out, local_sem.at[grad_written]).wait()
    arrived(grad_x_out, grad_x_slot)
    assert counts["send"] <= N_SEND and counts["recv"] <= N_RECV and counts["local"] <= N_LOCAL


def finish_kernel(down, normed, normed_x, grad, grad_x, up_out, down_out, n_own, n_x, g_own, g_x, moving, stage, sems):
    pairs = ((normed, n_own), (grad, g_own), (normed_x, n_x), (grad_x, g_x), (down, moving))
    loads = [pltpu.make_async_copy(src, dst, sems.at[i]) for i, (src, dst) in enumerate(pairs)]
    for copy in loads:
        copy.start()
    for copy in loads[:2]:
        copy.wait()
    for n in range(TILES):
        part = pl.ds(n * TILE, TILE)
        stage[part] = dot_first(n_own[:, part], g_own[...])
    for copy in loads[2:]:
        copy.wait()
    moved = pltpu.make_async_copy(moving, down_out, sems.at[0])
    moved.start()
    written = [moved]
    for n in range(TILES):
        part = pl.ds(n * TILE, TILE)
        stage[part] += dot_first(n_x[:, part], g_x[...])
        copy = pltpu.make_async_copy(stage.at[part], up_out.at[part], sems.at[5 + n])
        copy.start()
        written.append(copy)
    for copy in written:
        copy.wait()


def on_device(*args):
    any_ = pl.BlockSpec(memory_space=pl.ANY)
    vmem = pl.BlockSpec(memory_space=pltpu.VMEM)
    scratch = [
        ((2, W, W), bf16), ((2, W, W), bf16), ((2, W, W), bf16), ((2, W, W), bf16),
        ((2, OWN, W), bf16), ((2, OWN, W), f32), ((W,), f32), ((W,), f32), ((W,), f32),
        ((NY, OWN, 128), f32), ((NY, OWN, 128), f32),
        ((2, ROWS, W), bf16),
        ((2, 2 * GROUP, W), f32), ((NZ, 3, 2, OWN, W), bf16), ((NZ, 3, 2, OWN, W), bf16), ((NZ, 2, OWN, W), f32),
        ((2, ROWS, W), bf16), ((ROWS, W), bf16), ((NZ, OWN, W), bf16),
        ((2, 2, 2 * GROUP, W), f32), ((2, 2, 2, GROUP, W), bf16), ((2, 2, 2, GROUP, W), bf16),
        ((6, 2, 2, OWN, W), f32), ((6, 3, 2, 2, OWN, W), bf16), ((6, 3, 2, 2, OWN, W), bf16),
        ((5, 2, 2, OWN, W), bf16), ((5, 2, 2, OWN, W), bf16),
        ((2, ROWS, W), bf16), ((ROWS, W), bf16),
        ((2 * GROUP, W), f32), ((NZ, 3, OWN, W), bf16), ((NZ, 3, OWN, W), bf16), ((NZ, OWN, W), f32),
        ((ROWS, W), bf16), ((W, W), f32), ((2, W, W), bf16),
    ]
    product = jax.ShapeDtypeStruct((W, W), f32)
    rows = jax.ShapeDtypeStruct((ROWS, W), bf16)
    partial = pl.pallas_call(
        kernel,
        out_shape=(product, rows, rows, rows, rows),
        in_specs=[any_, vmem, vmem, any_, vmem, any_, vmem, any_, any_, any_],
        out_specs=(any_,) * 5,
        scratch_shapes=[pltpu.VMEM(shape, dtype) for shape, dtype in scratch]
        + [pltpu.SemaphoreType.DMA((N_SEND,)), pltpu.SemaphoreType.DMA((N_RECV,)), pltpu.SemaphoreType.DMA((N_LOCAL,))],
        compiler_params=pltpu.CompilerParams(
            collective_id=0, has_side_effects=True, vmem_limit_bytes=60 * 2**20
        ),
        cost_estimate=pl.CostEstimate(flops=9663676416, bytes_accessed=9437184, transcendentals=262144),
        name="gauss_newton",
    )(*args)
    return pl.pallas_call(
        finish_kernel,
        out_shape=(product, product),
        in_specs=[any_] * 5,
        out_specs=(any_, any_),
        scratch_shapes=[pltpu.VMEM((ROWS, W), bf16)] * 4
        + [pltpu.VMEM((W, W), f32)] * 2
        + [pltpu.SemaphoreType.DMA((8,))],
        compiler_params=pltpu.CompilerParams(vmem_limit_bytes=60 * 2**20),
        cost_estimate=pl.CostEstimate(flops=1207959552, bytes_accessed=10223616, transcendentals=0),
        name="finish",
    )(*partial)


def solution(mesh):
    return jax.shard_map(
        on_device,
        mesh=mesh,
        in_specs=(
            P("dp", "tensor"),
            P("tensor"),
            P("tensor"),
            P("tensor", "dp"),
            P("dp"),
            P("dp", "tensor"),
            P("tensor"),
            P("dp", "tensor"),
            P("tensor", "dp"),
            P("dp", "tensor"),
        ),
        out_specs=(P("tensor", "dp"), P("dp", "tensor")),
        check_vma=False,
    )
```

```python
import functools

import jax
import jax.numpy as jnp
from jax import lax
from jax.experimental import pallas as pl
from jax.experimental.pallas import tpu as pltpu
from jax.sharding import PartitionSpec as P

D = 6144
epsilon = 1e-05
root_half = 0.7071067811865476
inv_root_two_pi = 0.3989422804014327

f32 = jnp.float32
bf16 = jnp.bfloat16
MESH = pl.DeviceIdType.MESH

NX, NZ, NY = 4, 8, 4
OWN = 16
GROUP = NX * OWN
ROWS = NZ * GROUP
W = 768
TILE = 256
TILES = W // TILE
FORWARD = {"0": (0,), "4": (4,), "17": (1, 7), "3": (3,), "5": (5,), "2": (2,), "6": (6,)}
BACKWARD = {"0": (0,), "17": (1, 7), "6": (6,), "2": (2,), "5": (5,), "3": (3,), "4": (4,)}
NEAR = (1, 7)
FAR = (4, 3, 5, 2, 6)
J_ORDER = (2, 1, 3)

N_SEND = 22
N_RECV = 94
N_LOCAL = 15


def dot(a, b):
    return jnp.dot(a, b, preferred_element_type=f32)


def dot_last(a, b):
    return lax.dot_general(a, b, (((1,), (1,)), ((), ())), preferred_element_type=f32)


def dot_first(a, b):
    return lax.dot_general(a, b, (((0,), (0,)), ((), ())), preferred_element_type=f32)


def columns(values):
    lane = lax.broadcasted_iota(jnp.int32, (OWN, 128), 1)
    out = jnp.zeros((OWN, 128), f32)
    for at, value in enumerate(values):
        out = jnp.where(lane == at, value, out)
    return out


def row_sum(pair):
    return jnp.sum(pair[0] + pair[1], axis=1, keepdims=True)


def kernel(
    tokens, gain_in_at, shift_in_at, up_weight, up_bias_at, down_weight, gain_out_at, curvature, up_tangent, down_tangent,
    down_out, normed_out, normed_x_out, grad_out, grad_x_out,
    w_up, w_ut, w_dn, w_dt, tok, curv, gin_x, sin_x, gout_x,
    stat_a, stat_b, normed, part_f, part_s, part_r, part_own,
    both, hidden_x, slope, out_f, raw_s, raw_r, own_x, out_s, out_r, sum_s, sum_r,
    cot, cot_x, back_f, back_s, back_r, back_own, grad, stage, w_dn_t,
    gain_in, shift_in, gain_out, up_bias,
    send_sem, recv_sem, local_sem,
):
    d, t = lax.axis_index("dp"), lax.axis_index("tensor")
    x, z = d // NZ, lax.rem(d, NZ)
    y, c = t // 2, lax.rem(t, 2)
    other = 1 - c

    def at_x(k):
        return (lax.rem(x + k, NX) * NZ + z, t)

    def at_z(k):
        return (x * NZ + lax.rem(z + k, NZ), t)

    def at_y(k):
        return (d, lax.rem(y + k, NY) * 2 + c)

    sibling = (d, y * 2 + other)
    ends, counts = [], {"send": 0, "recv": 0, "local": 0}

    def fresh(kind, n=1):
        at = counts[kind]
        counts[kind] += n
        return at

    def sends_of(ref):
        slot = fresh("send")
        ends.append((ref, slot))
        return slot

    def copy_to(src, dst, device, sent, slot):
        pltpu.make_async_remote_copy(
            src_ref=src, dst_ref=dst, send_sem=send_sem.at[sent],
            recv_sem=recv_sem.at[slot], device_id=device, device_id_type=MESH,
        ).start()

    def bytes_of(ref, sent, slot):
        return pltpu.make_async_remote_copy(
            src_ref=ref, dst_ref=ref, send_sem=send_sem.at[sent],
            recv_sem=recv_sem.at[slot], device_id=sibling, device_id_type=MESH,
        )

    def arrived(ref, slot):
        bytes_of(ref, 0, slot).wait_recv()

    def copy_here(src, dst):
        copy = pltpu.make_async_copy(src, dst, local_sem.at[fresh("local")])
        copy.start()
        return copy

    barrier = pltpu.get_barrier_semaphore()
    peers = [sibling] + [at_x(k) for k in range(1, NX)] + [at_z(k) for k in range(1, NZ)] + [at_y(k) for k in range(1, NY)]
    for peer in peers:
        pl.semaphore_signal(barrier, inc=1, device_id=peer, device_id_type=MESH)
    own_rows = pl.ds(pl.multiple_of(c * OWN, OWN), OWN)
    their_rows = pl.ds(pl.multiple_of(other * OWN, OWN), OWN)
    tok_here = copy_here(tokens.at[own_rows], tok.at[c])
    vectors = ((gain_in_at, gain_in), (shift_in_at, shift_in), (gain_out_at, gain_out), (up_bias_at, up_bias))
    vectors_here = [copy_here(src, dst) for src, dst in vectors]
    curv_here = copy_here(curvature.at[own_rows], curv.at[c])
    up_here = [copy_here(up_weight, w_up.at[c]), copy_here(up_tangent, w_ut.at[c])]
    down_here = [copy_here(down_weight, w_dn.at[c]), copy_here(down_tangent, w_dt.at[c])]
    pl.semaphore_wait(barrier, len(peers))

    tok_slot, params_slot, curv_slot = fresh("recv"), fresh("recv", 3), fresh("recv")
    up_slot, down_slot = fresh("recv"), fresh("recv")
    copy_to(tokens.at[their_rows], tok.at[c], sibling, sends_of(tok.at[c]), tok_slot)
    for copy in vectors_here:
        copy.wait()
    for i, (mine, theirs) in enumerate(((gain_in, gin_x), (shift_in, sin_x), (gain_out, gout_x))):
        copy_to(mine, theirs, sibling, sends_of(theirs), params_slot + i)

    def send_weights(pairs, whole, slot):
        sent = sends_of(whole)
        for mine, theirs in pairs:
            copy_to(mine, theirs.at[c], sibling, sent, slot)

    tok_here.wait()
    arrived(tok.at[other], tok_slot)
    source = tok[...].astype(f32)
    total = row_sum(source)
    spread = source - (total / (2 * W))[None]
    stat_a[0] = columns([total, row_sum(spread * spread)])
    stat_slot, sent = fresh("recv"), sends_of(stat_a.at[pl.ds(1, 3)])
    for k in J_ORDER:
        copy_to(stat_a.at[0], stat_a.at[k], at_y(k), sent, stat_slot)
    arrived(gin_x, params_slot)
    arrived(sin_x, params_slot + 1)
    arrived(gout_x, params_slot + 2)

    def by_half(mine, theirs):
        mine, theirs = mine[...].reshape(1, W), theirs[...].reshape(1, W)
        first = jnp.where(c == 0, mine, theirs)
        second = jnp.where(c == 0, theirs, mine)
        return jnp.stack([first, second])

    gain, shift = by_half(gain_in, gin_x), by_half(shift_in, sin_x)
    arrived(stat_a.at[pl.ds(1, 3)], stat_slot)
    totals = [stat_a[k][:, 0:1] for k in range(NY)]
    center = (totals[0] + totals[1] + totals[2] + totals[3]) / D
    variance = jnp.zeros_like(center)
    for k in range(NY):
        off = totals[k] / (2 * W) - center
        variance = variance + stat_a[k][:, 1:2] + (2 * W) * (off * off)
    inverse = lax.rsqrt(variance / D + epsilon)
    def group(k):
        return pl.ds(pl.multiple_of(lax.rem(z + NZ + k, NZ) * GROUP, GROUP), GROUP)

    def block_of(j, k):
        first = lax.rem(z + NZ + k, NZ) * GROUP + lax.rem(x + NX + j, NX) * OWN
        return pl.ds(pl.multiple_of(first, OWN), OWN)

    block = block_of(0, 0)
    normed[:, block] = ((source - center[None]) * inverse[None] * gain + shift).astype(bf16)

    def three_of(offset):
        first = lax.rem(z + NZ + offset, NZ) * GROUP
        return pl.ds(pl.multiple_of(first, GROUP), GROUP - OWN)

    def gather_start(array, far, between, relay):
        sent = sends_of(array.at[:, pl.ds(0, ROWS - OWN)])

        def send(rows, device, slot):
            copy_to(array.at[:, rows], array.at[:, rows], device, sent, slot)

        z_slot, x_slot, last_slot = fresh("recv", NZ), fresh("recv", NX), fresh("recv", NZ)
        for j in J_ORDER:
            send(block, at_x(j), x_slot + j)
        for k in (4,) + NEAR if relay else NEAR + far:
            send(block, at_z(k), z_slot + k)
        between()
        for k, onward in ((1, ((1, 2), (2, 3))), (7, ((7, 6), (6, 5)))):
            rows = block_of(0, -k)
            arrived(array.at[:, rows], z_slot + k)
            for step, total in onward if relay else ():
                send(rows, at_z(step), z_slot + total)
        for j in (1, 3, 2):
            rows = block_of(-j, 0)
            arrived(array.at[:, rows], x_slot + j)
            for k in NEAR:
                send(rows, at_z(k), last_slot + k)
        for k in far:
            rows = block_of(0, -k)
            arrived(array.at[:, rows], z_slot + k)
            for j in J_ORDER:
                send(rows, at_x(j), last_slot + k)
        return last_slot

    def gather_wait(array, last_slot, chunk):
        for offset in chunk:
            k = (NZ - offset) % NZ
            if k in NEAR:
                arrived(array.at[:, three_of(-k)], last_slot + k)
            elif k:
                arrived(array.at[:, three_of(-k)], last_slot + k)

    def stacked(array, chunk):
        parts = [array[group(offset)] for offset in chunk]
        return parts[0] if len(parts) == 1 else jnp.concatenate(parts, axis=0)

    normed_slots = gather_start(
        normed, (4, 3, 5, 2, 6), lambda: send_weights(((up_weight, w_up), (up_tangent, w_ut)), w_up, up_slot), True
    )
    send_weights(((down_weight, w_dn), (down_tangent, w_dt)), w_dn, down_slot)
    copy_to(curvature.at[their_rows], curv.at[c], sibling, sends_of(curv.at[c]), curv_slot)

    share_slot, share_sent = fresh("recv", NZ), sends_of(part_s)
    both_slot, both_sent = fresh("recv", NZ), sends_of(both.at[:, pl.ds(0, ROWS - NZ * OWN)])
    normed_x_slot, hidden_x_slot = fresh("recv"), fresh("recv")
    raw_slot, raw_sent = fresh("recv", 2), sends_of(raw_s)
    out_slot, out_sent = fresh("recv", 6), sends_of(out_s)
    sum_slot, sum_sent = fresh("recv"), sends_of(sum_s)
    ordered = (0,) + FAR

    def up_step(name):
        chunk = FORWARD[name]
        size = len(chunk)
        gather_wait(normed, normed_slots, chunk)
        if up_here:
            while up_here:
                up_here.pop().wait()
            arrived(w_up, up_slot)
        left, right = stacked(normed.at[0], chunk), stacked(normed.at[1], chunk)
        rows = pl.ds(0, size * GROUP)
        part_f[0, rows] = dot(left, w_up[0]) + dot(right, w_up[1])
        part_f[1, rows] = dot(left, w_ut[0]) + dot(right, w_ut[1])

        def share(i, j):
            mine = lax.rem(y + j, NY) * OWN
            return part_f[:, pl.ds(pl.multiple_of(i * GROUP + mine, OWN), OWN)]

        for j in J_ORDER:
            for i, offset in enumerate(chunk):
                part_s[offset, j - 1] = share(i, j).astype(bf16)
                copy_to(part_s.at[offset, j - 1], part_r.at[offset, j - 1], at_y(j), share_sent, share_slot + offset)
        for i, offset in enumerate(chunk):
            part_own[offset] = share(i, 0)

    def share_rows(offset, who):
        first = lax.rem(z + offset, NZ) * GROUP + lax.rem(who + NY, NY) * OWN
        return pl.ds(pl.multiple_of(first, OWN), OWN)

    def act_step(name):
        for offset in FORWARD[name]:
            arrived(part_r.at[offset], share_slot + offset)
            sums = part_own[offset]
            for j in range(1, NY):
                sums = sums + part_r[offset, j - 1].astype(f32)
            pre = sums[0] + up_bias[...].reshape(1, W)
            phi = 0.5 * (1.0 + lax.erf(pre * root_half))
            derivative = phi + pre * jnp.exp(-0.5 * pre * pre) * inv_root_two_pi
            rows = share_rows(offset, y)
            both[0, rows] = (pre * phi).astype(bf16)
            both[1, rows] = (derivative * sums[1]).astype(bf16)
            slope[offset] = derivative.astype(bf16)
            for j in J_ORDER:
                copy_to(both.at[:, rows], both.at[:, rows], at_y(j), both_sent, both_slot + offset)

    def down_step(name):
        chunk = FORWARD[name]
        for offset in chunk:
            arrived(both.at[:, three_of(offset)], both_slot + offset)
        if down_here:
            while down_here:
                down_here.pop().wait()
            arrived(w_dn, down_slot)
        hidden, hidden_tangent = stacked(both.at[0], chunk), stacked(both.at[1], chunk)
        rows = pl.ds(0, len(chunk) * GROUP)
        for f in range(2):
            out_f[0, f, rows] = dot(hidden, w_dn[f])
            out_f[1, f, rows] = dot(hidden_tangent, w_dn[f]) + dot(hidden, w_dt[f])
        for i, offset in enumerate(chunk):
            if offset in NEAR:
                at = NEAR.index(offset)
                raw_s[at] = out_f[:, :, pl.ds(i * GROUP, GROUP)].astype(bf16)
                copy_to(raw_s.at[at], raw_r.at[at], at_z(offset), raw_sent, raw_slot + at)
                continue
            at = ordered.index(offset)
            if offset == 0:
                for k in range(len(NEAR)):
                    arrived(raw_r.at[k], raw_slot + k)

            def part(j):
                first = pl.multiple_of(lax.rem(x + j, NX) * OWN, OWN)
                value = out_f[:, :, pl.ds(first, OWN)]
                if offset == 0:
                    for k in range(len(NEAR)):
                        value = value + raw_r[k, :, :, pl.ds(first, OWN)].astype(f32)
                return value

            for j in J_ORDER:
                out_s[at, j - 1] = part(j).astype(bf16)
                copy_to(out_s.at[at, j - 1], out_r.at[at, j - 1], at_x(j), out_sent, out_slot + at)
            own_x[at] = part(0)

    def summed(offset):
        at = ordered.index(offset)
        arrived(out_r.at[at], out_slot + at)
        value = own_x[at]
        for j in range(1, NX):
            value = value + out_r[at, j - 1].astype(f32)
        return value

    def sum_step(name):
        for offset in FORWARD[name]:
            at = FAR.index(offset)
            sum_s[at] = summed(offset).astype(bf16)
            copy_to(sum_s.at[at], sum_r.at[at], at_z(offset), sum_sent, sum_slot)

    steps = {"u": up_step, "a": act_step, "d": down_step, "s": sum_step}
    order = (
        "u0", "u17", "u4", "u3", "a17", "a4", "u5", "a3", "d17", "d4", "u2", "a5", "d3",
        "u6", "a2", "d5", "s4", "a6", "s3", "a0", "d2", "s5", "d6", "s2", "d0", "s6",
    )
    for step in order:
        if step == "d2":
            copy_to(normed.at[other], normed_x_out, sibling, sends_of(normed.at[other]), normed_x_slot)
            normed_written = copy_here(normed.at[c], normed_out)
            for f in range(2):
                w_dn_t[f] = w_dn[f].T
        steps[step[0]](step[1:])
    copy_to(both.at[0], hidden_x, sibling, sends_of(both.at[0]), hidden_x_slot)

    arrived(curv.at[other], curv_slot)
    curv_here.wait()
    gain = by_half(gain_out, gout_x)
    factor = gain * gain * curv[...]
    outputs = summed(0)
    arrived(sum_r, sum_slot)
    for k in range(len(FAR)):
        outputs = outputs + sum_r[k].astype(f32)

    output = tok[...].astype(f32) + outputs[0]
    tangent = outputs[1]
    total = row_sum(output)
    around = output - (total / (2 * W))[None]
    factor_around = factor * around
    stat_b[0] = columns([
        total, row_sum(around * around), row_sum(tangent), row_sum(around * tangent),
        row_sum(factor), row_sum(factor_around), row_sum(factor_around * around),
        row_sum(factor * tangent), row_sum(factor_around * tangent),
    ])
    stat_slot, sent = fresh("recv"), sends_of(stat_b.at[pl.ds(1, 3)])
    for k in J_ORDER:
        copy_to(stat_b.at[0], stat_b.at[k], at_y(k), sent, stat_slot)
    arrived(stat_b.at[pl.ds(1, 3)], stat_slot)
    stats = [[stat_b[k][:, i:i + 1] for i in range(9)] for k in range(NY)]
    center = (stats[0][0] + stats[1][0] + stats[2][0] + stats[3][0]) / D
    zero = jnp.zeros_like(center)
    square, sum_t, dot_t, f_0, f_1, f_2, ft_0, ft_1 = (zero,) * 8
    for s in stats:
        off = s[0] / (2 * W) - center
        square = square + s[1] + (2 * W) * (off * off)
        sum_t = sum_t + s[2]
        dot_t = dot_t + s[3] + off * s[2]
        f_0 = f_0 + s[4]
        f_1 = f_1 + s[5] + off * s[4]
        f_2 = f_2 + s[6] + 2.0 * off * s[5] + off * off * s[4]
        ft_0 = ft_0 + s[7]
        ft_1 = ft_1 + s[8] + off * s[7]
    inverse = lax.rsqrt(square / D + epsilon)
    mean_t = sum_t / D
    mean_nt = dot_t * inverse / D
    fn_1 = f_1 * inverse
    mean_w = (ft_0 - mean_t * f_0 - mean_nt * fn_1) * inverse / D
    mean_nw = (ft_1 * inverse - mean_t * fn_1 - mean_nt * (f_2 * inverse * inverse)) * inverse / D
    normal = (output - center[None]) * inverse[None]
    weighted = factor * ((tangent - mean_t[None] - normal * mean_nt[None]) * inverse[None])
    cot[:, block] = ((weighted - mean_w[None] - normal * mean_nw[None]) * inverse[None]).astype(bf16)

    cot_slots = gather_start(cot, FAR[::-1], lambda: None, False)
    back_slot, back_sent = fresh("recv", NZ), sends_of(back_s)
    grad_slot, grad_sent = fresh("recv", NZ), sends_of(grad.at[pl.ds(0, ROWS - NZ * OWN)])
    cot_x_slot, cot_x_sent = fresh("recv"), sends_of(cot.at[other])
    grad_x_slot, grad_x_sent = fresh("recv"), sends_of(grad)
    grad_written = fresh("local")

    def back_step(name):
        chunk = BACKWARD[name]
        size = len(chunk)
        gather_wait(cot, cot_slots, chunk)
        left, right = stacked(cot.at[0], chunk), stacked(cot.at[1], chunk)
        back_f[pl.ds(0, size * GROUP)] = dot(left, w_dn_t[0]) + dot(right, w_dn_t[1])

        def share(i, j):
            mine = lax.rem(y + j, NY) * OWN
            return back_f[pl.ds(pl.multiple_of(i * GROUP + mine, OWN), OWN)]

        for j in J_ORDER:
            for i, offset in enumerate(chunk):
                back_s[offset, j - 1] = share(i, j).astype(bf16)
                copy_to(back_s.at[offset, j - 1], back_r.at[offset, j - 1], at_y(j), back_sent, back_slot + offset)
        for i, offset in enumerate(chunk):
            back_own[offset] = share(i, 0)
            rows = group(offset)
            copy_to(cot.at[other, rows], cot_x.at[rows], sibling, cot_x_sent, cot_x_slot)

    def grad_step(name):
        for offset in BACKWARD[name]:
            arrived(back_r.at[offset], back_slot + offset)
            sums = back_own[offset]
            for j in range(1, NY):
                sums = sums + back_r[offset, j - 1].astype(f32)
            rows = share_rows(offset, y)
            grad[rows] = (sums * slope[offset].astype(f32)).astype(bf16)
            for j in J_ORDER:
                copy_to(grad.at[rows], grad.at[rows], at_y(j), grad_sent, grad_slot + offset)

    def swap_step(name):
        for offset in BACKWARD[name]:
            arrived(grad.at[three_of(offset)], grad_slot + offset)
            rows = group(offset)
            copy_to(grad.at[rows], grad_x_out.at[rows], sibling, grad_x_sent, grad_x_slot)
            copy = pltpu.make_async_copy(grad.at[rows], grad_out.at[rows], local_sem.at[grad_written])
            copy.start()

    written = [normed_written]

    def product_step(_):
        arrived(hidden_x, hidden_x_slot)
        arrived(cot_x, cot_x_slot)
        for n in range(TILES):
            part = pl.ds(n * TILE, TILE)
            stage[part] = dot_first(both[0, :, part], cot[c]) + dot_first(hidden_x[:, part], cot_x[...])
            written.append(copy_here(stage.at[part], down_out.at[part]))

    steps = {"b": back_step, "g": grad_step, "w": swap_step, "p": product_step}
    order = (
        "b0", "b17", "b6", "g0", "b2", "g17", "b5", "g6", "b3", "g2", "b4", "g5",
        "g3", "g4", "w0", "w17", "w6", "p", "w2", "w5", "w3", "w4",
    )
    for step in order:
        steps[step[0]](step[1:])
    arrived(normed_x_out, normed_x_slot)
    for copy in written:
        copy.wait()
    for ref, slot in ends:
        bytes_of(ref, slot, 0).wait_send()
    pltpu.make_async_copy(grad, grad_out, local_sem.at[grad_written]).wait()
    arrived(grad_x_out, grad_x_slot)
    assert counts["send"] <= N_SEND and counts["recv"] <= N_RECV and counts["local"] <= N_LOCAL


def finish_kernel(down, normed, normed_x, grad, grad_x, up_out, down_out, n_own, n_x, g_own, g_x, moving, stage, sems):
    pairs = ((normed, n_own), (grad, g_own), (normed_x, n_x), (grad_x, g_x), (down, moving))
    loads = [pltpu.make_async_copy(src, dst, sems.at[i]) for i, (src, dst) in enumerate(pairs)]
    for copy in loads:
        copy.start()
    for copy in loads[:2]:
        copy.wait()
    for n in range(TILES):
        part = pl.ds(n * TILE, TILE)
        stage[part] = dot_first(n_own[:, part], g_own[...])
    for copy in loads[2:]:
        copy.wait()
    moved = pltpu.make_async_copy(moving, down_out, sems.at[0])
    moved.start()
    written = [moved]
    for n in range(TILES):
        part = pl.ds(n * TILE, TILE)
        stage[part] += dot_first(n_x[:, part], g_x[...])
        copy = pltpu.make_async_copy(stage.at[part], up_out.at[part], sems.at[5 + n])
        copy.start()
        written.append(copy)
    for copy in written:
        copy.wait()


def on_device(*args):
    any_ = pl.BlockSpec(memory_space=pl.ANY)
    scratch = [
        ((2, W, W), bf16), ((2, W, W), bf16), ((2, W, W), bf16), ((2, W, W), bf16),
        ((2, OWN, W), bf16), ((2, OWN, W), f32), ((W,), f32), ((W,), f32), ((W,), f32),
        ((NY, OWN, 128), f32), ((NY, OWN, 128), f32),
        ((2, ROWS, W), bf16),
        ((2, 2 * GROUP, W), f32), ((NZ, 3, 2, OWN, W), bf16), ((NZ, 3, 2, OWN, W), bf16), ((NZ, 2, OWN, W), f32),
        ((2, ROWS, W), bf16), ((ROWS, W), bf16), ((NZ, OWN, W), bf16),
        ((2, 2, 2 * GROUP, W), f32), ((2, 2, 2, GROUP, W), bf16), ((2, 2, 2, GROUP, W), bf16),
        ((6, 2, 2, OWN, W), f32), ((6, 3, 2, 2, OWN, W), bf16), ((6, 3, 2, 2, OWN, W), bf16),
        ((5, 2, 2, OWN, W), bf16), ((5, 2, 2, OWN, W), bf16),
        ((2, ROWS, W), bf16), ((ROWS, W), bf16),
        ((2 * GROUP, W), f32), ((NZ, 3, OWN, W), bf16), ((NZ, 3, OWN, W), bf16), ((NZ, OWN, W), f32),
        ((ROWS, W), bf16), ((W, W), f32), ((2, W, W), bf16),
        ((W,), f32), ((W,), f32), ((W,), f32), ((W,), f32),
    ]
    product = jax.ShapeDtypeStruct((W, W), f32)
    rows = jax.ShapeDtypeStruct((ROWS, W), bf16)
    partial = pl.pallas_call(
        kernel,
        out_shape=(product, rows, rows, rows, rows),
        in_specs=[any_] * 10,
        out_specs=(any_,) * 5,
        scratch_shapes=[pltpu.VMEM(shape, dtype) for shape, dtype in scratch]
        + [pltpu.SemaphoreType.DMA((N_SEND,)), pltpu.SemaphoreType.DMA((N_RECV,)), pltpu.SemaphoreType.DMA((N_LOCAL,))],
        compiler_params=pltpu.CompilerParams(
            collective_id=0, has_side_effects=True, vmem_limit_bytes=60 * 2**20
        ),
        cost_estimate=pl.CostEstimate(flops=9663676416, bytes_accessed=9437184, transcendentals=262144),
        name="gauss_newton",
    )(*args)
    return pl.pallas_call(
        finish_kernel,
        out_shape=(product, product),
        in_specs=[any_] * 5,
        out_specs=(any_, any_),
        scratch_shapes=[pltpu.VMEM((ROWS, W), bf16)] * 4
        + [pltpu.VMEM((W, W), f32)] * 2
        + [pltpu.SemaphoreType.DMA((8,))],
        compiler_params=pltpu.CompilerParams(vmem_limit_bytes=60 * 2**20),
        cost_estimate=pl.CostEstimate(flops=1207959552, bytes_accessed=10223616, transcendentals=0),
        name="finish",
    )(*partial)


def solution(mesh):
    return jax.shard_map(
        on_device,
        mesh=mesh,
        in_specs=(
            P("dp", "tensor"),
            P("tensor"),
            P("tensor"),
            P("tensor", "dp"),
            P("dp"),
            P("dp", "tensor"),
            P("tensor"),
            P("dp", "tensor"),
            P("tensor", "dp"),
            P("dp", "tensor"),
        ),
        out_specs=(P("tensor", "dp"), P("dp", "tensor")),
        check_vma=False,
    )
```
